32 devices in a mesh: dp: 8 (over z, x), fsdp: 4 (over y, core).
Axes of the slice: x: 2, y: 2, z: 4, core: 2. Of those that a mesh axis runs over, the one named last changes fastest.
Arguments:
- hidden_states: bfloat16 [4096, 8192], P(('dp', 'fsdp')), may hold values from -450 to 450
- gain: float32 [8192], replicated, may hold values from 0.1 to 1.9
- key_weight: bfloat16 [8192, 512], P('fsdp'), may hold values from -0.0625 to 0.0625
- key_cotangent: bfloat16 [4096, 512], P(('dp', 'fsdp')), may hold values from -18 to 18
- bucket: int32 [5, 32768], P(None, 'fsdp'), may hold values from 0 to 255
- sign_bits: int32 [5, 32768], P(None, 'fsdp'), may hold values from 0 to 1
- momentum: float32 [4, 5, 32768], P('fsdp', None, 'dp'), may hold values from -12 to 12
- error: float32 [4, 5, 32768], P('fsdp', None, 'dp'), may hold values from -12 to 12
Outputs:
- hidden_grad: bfloat16 [4096, 8192], P(('dp', 'fsdp'))
- momentum_new: float32 [4, 5, 32768], P('fsdp', None, 'dp')
- error_new: float32 [4, 5, 32768], P('fsdp', None, 'dp')
- update: float32 [8192, 512], P('fsdp')
The draws below stay inside these ranges and needn't reach their ends.
All inputs are finite; a program needn't handle non-finite values.
Results may differ from the reference program's by a relative error of at most 0.0095.
Values may be sent and summed in bfloat16 or wider, within the bound.
No kernel may reach another device: no remote copies, remote signals or barrier semaphores. Data moves between devices by JAX's collectives and lax.ppermute only.
A program may use at most 128 MiB of HBM per device.

```python
import math
import jax
import jax.numpy as jnp
from jax import lax

D = 8192
ROWS = 5
NBB = 256
BLOCK = 128
KEY_WIDTH = 512
GROUP = 512
TOKENS = 4096
NBLK = 32768
BUCKETS = 32768
TABLES = 4
N_DP = 8
N_FSDP = 4


def draw_hidden_states(key, part):
    keys = jax.random.split(key, 3)
    base = jnp.clip(jax.random.normal(keys[0], (TOKENS, D), jnp.float32), -4.0, 4.0)
    row_scale = jnp.exp(jax.random.uniform(keys[1], (TOKENS, 1), jnp.float32, 0.0, math.log(10.0)))
    col_scale = jnp.exp(jax.random.uniform(keys[2], (1, D), jnp.float32, 0.0, math.log(10.0)))
    return (base * row_scale * col_scale).astype(jnp.bfloat16)


def set_ends(result, rng, low, high):
    extent = result.shape
    spot = [jax.random.randint(jax.random.fold_in(rng, axis), (), 0, extent[axis]) for axis in range(len(extent))]
    result = result.at[tuple(spot)].set(low)
    longest = extent.index(max(extent))
    spot[longest] = (spot[longest] + 1) % extent[longest]
    return result.at[tuple(spot)].set(high)


def level_of(key, extent, cuts, low, top_value):
    def one(axis_at, blocks):
        steps = jax.random.uniform(jax.random.fold_in(jax.random.fold_in(key, 6), axis_at), (blocks,), jnp.float32, low / len(cuts), top_value / len(cuts))
        return jnp.repeat(jnp.exp(steps), extent[axis_at] // blocks).reshape((-1,) + (1,) * (len(extent) - axis_at - 1))

    factor_of = one(*cuts[0])
    for cut in cuts[1:]:
        factor_of = factor_of * one(*cut)
    return factor_of


def bell_draw(own_key, extent, spread, limit, cuts=(), kind=jnp.bfloat16):
    result = jax.random.normal(own_key, extent, jnp.float32) * spread
    if len(cuts) > 0:
        result = level_of(own_key, extent, cuts, -0.22, 0.18) * result
    return jnp.clip(result, min=-limit, max=limit).astype(kind)


def setup_inputs(seed: int = 0) -> dict:
    key_list = jax.random.split(jax.random.key(seed), 9)
    return {
        "hidden_states": draw_hidden_states(jax.random.fold_in(key_list[8], 71), 0),
        "gain": jnp.clip(1.0 + 0.18 * jax.random.normal(key_list[1], (D,), jnp.float32), 0.1, 1.9),
        "key_weight": bell_draw(key_list[2], (D, KEY_WIDTH), D ** -0.5, 0.0625, ((0, 4),)),
        "key_cotangent": bell_draw(key_list[3], (TOKENS, KEY_WIDTH), 3.0, 18.0, ((0, 32),)),
        "bucket": set_ends(jax.random.randint(key_list[4], (ROWS, NBLK), 0, NBB), jax.random.fold_in(key_list[4], 1), 0, NBB - 1).astype(jnp.int32),
        "sign_bits": set_ends(jax.random.randint(key_list[5], (ROWS, NBLK), 0, 2), jax.random.fold_in(key_list[5], 1), 0, 1).astype(jnp.int32),
        "momentum": bell_draw(key_list[6], (TABLES, ROWS, BUCKETS), 2.0, 12.0, ((0, 4), (2, 8)), jnp.float32),
        "error": bell_draw(key_list[7], (TABLES, ROWS, BUCKETS), 2.0, 12.0, ((0, 4), (2, 8)), jnp.float32),
    }


EPS = 1e-05
DECAY = 0.9
THRESHOLD = 1.0

def normalize(states, gain):
    values = states.astype(jnp.float32)
    inverse_rms = lax.rsqrt(lax.optimization_barrier(jnp.mean(values * values, axis=1, keepdims=True)) + EPS)
    normed = values * inverse_rms
    return (normed, inverse_rms, (normed * gain).astype(jnp.bfloat16))

def norm_backward(input_grad, gain, normed, inverse_rms):
    scaled = input_grad.astype(jnp.float32) * gain
    mean_term = lax.optimization_barrier(jnp.mean(scaled * normed, axis=1, keepdims=True))
    return (inverse_rms * (scaled - normed * mean_term)).astype(jnp.bfloat16)

def sketch(blocks, bucket, signs):
    slab = jnp.arange(NBLK, dtype=jnp.int32) // (NBLK // N_FSDP)
    seg_ids = (slab[None, :] * NBB + bucket).astype(jnp.int32)
    tables = jnp.stack([jax.ops.segment_sum(signs[k][:, None] * blocks, seg_ids[k], num_segments=N_FSDP * NBB) for k in range(ROWS)])
    return tables.reshape(ROWS, N_FSDP, NBB * BLOCK).transpose(1, 0, 2)

def reference(hidden_states, gain, key_weight, key_cotangent, bucket, sign_bits, momentum, error):
    signs = (2 * sign_bits - 1).astype(jnp.float32)
    grad_scale = 1.0 / math.sqrt(GROUP)

    def one_group(pair):
        states, cotangent = pair
        normed, inverse_rms, inputs = normalize(states, gain)
        input_grad = jnp.dot(cotangent, key_weight.T, preferred_element_type=jnp.float32).astype(jnp.bfloat16)
        group_grad = norm_backward(input_grad, gain, normed, inverse_rms)
        weight_grad = jnp.dot(inputs.T, cotangent, preferred_element_type=jnp.float32) * grad_scale
        return (group_grad, sketch(weight_grad.reshape(NBLK, BLOCK), bucket, signs))
    grads, tables = lax.map(one_group, (hidden_states.reshape(N_DP, GROUP, D), key_cotangent.reshape(N_DP, GROUP, KEY_WIDTH)))
    mean_table = lax.optimization_barrier(jnp.sum(tables, axis=0)) / N_DP
    momentum_new = DECAY * momentum + mean_table
    error_sum = error + momentum_new
    error_blocks = error_sum.reshape(N_FSDP, ROWS, NBB, BLOCK)
    slab = jnp.arange(NBLK, dtype=jnp.int32) // (NBLK // N_FSDP)
    row_ids = jnp.arange(ROWS, dtype=jnp.int32)
    reads = error_blocks[slab[None, :], row_ids[:, None], bucket] * signs[:, :, None]
    estimate = jnp.sort(reads, axis=0)[ROWS // 2]
    update = estimate - jnp.clip(estimate, -THRESHOLD, THRESHOLD)
    error_new = error_sum - sketch(update, bucket, signs)
    return (grads.reshape(TOKENS, D), momentum_new, error_new, update.reshape(D, KEY_WIDTH))
```

```python
import functools
import math

import jax
import jax.numpy as jnp
from jax import lax
from jax.experimental import pallas as pl
from jax.experimental.pallas import tpu as pltpu
from jax.sharding import PartitionSpec as P

ROWS = 5
NBB = 256
BLOCK = 128
PAD = 8

EPS = 1e-05
DECAY = 0.9
THRESHOLD = 1.0
MIB = 1024 * 1024


def params(limit=48):
    return pltpu.CompilerParams(vmem_limit_bytes=limit * MIB)


def middle_three(first, second, third):
    return jnp.maximum(jnp.minimum(first, second), jnp.minimum(jnp.maximum(first, second), third))


def middle_five(items):
    upper_pair = jnp.minimum(jnp.maximum(items[0], items[1]), jnp.maximum(items[2], items[3]))
    lower_pair = jnp.maximum(jnp.minimum(items[0], items[1]), jnp.minimum(items[2], items[3]))
    return middle_three(items[4], upper_pair, lower_pair)


def partner(index, step, count):
    if count & (count - 1) == 0:
        return index ^ step
    return (index + step) % count


def turn(index, step, count):
    return (index + step) % count


def prep_kernel(where, bucket_ref, sign_ref, rows_ref, cols_ref, stacked):
    share, count = where[1], where[2]
    quads = rows_ref.shape[0]
    width = quads * BLOCK
    groups = bucket_ref.shape[1] // width
    bucket = bucket_ref[...]
    bucket = jnp.where(count == 1, bucket ^ share, lax.rem(bucket + (NBB - share), NBB))
    code = ((bucket + 1) * (2 * sign_ref[...] - 1)).astype(jnp.float32)
    stacked[...] = jnp.zeros_like(stacked)
    for group in range(groups):
        stacked[group * PAD : group * PAD + ROWS, :] = code[:, group * width : (group + 1) * width]
    source = lax.broadcasted_iota(jnp.int32, (width, width), 0)
    target = lax.broadcasted_iota(jnp.int32, (width, width), 1)
    chosen = source == quads * (target % BLOCK) + target // BLOCK
    order = jnp.where(chosen, 1.0, 0.0).astype(jnp.bfloat16)
    moved = jnp.dot(stacked[...].astype(jnp.bfloat16), order, preferred_element_type=jnp.float32)
    for group in range(groups):
        for quad in range(quads):
            rows_ref[quad, :, group * BLOCK : (group + 1) * BLOCK] = moved[
                group * PAD : (group + 1) * PAD, quad * BLOCK : (quad + 1) * BLOCK
            ].astype(rows_ref.dtype)
    for quad in range(quads):
        cols_ref[:, quad * PAD : (quad + 1) * PAD] = (
            rows_ref[quad].astype(jnp.float32).T
        )


def prep(where, bucket, sign_bits, quads):
    blocks = bucket.shape[1]
    features = blocks // quads
    vmem = pl.BlockSpec(memory_space=pltpu.VMEM)
    return pl.pallas_call(
        prep_kernel,
        out_shape=(
            jax.ShapeDtypeStruct((quads, PAD, features), jnp.bfloat16),
            jax.ShapeDtypeStruct((features, quads * PAD), jnp.float32),
        ),
        in_specs=[pl.BlockSpec(memory_space=pltpu.SMEM), vmem, vmem],
        out_specs=(vmem, vmem),
        scratch_shapes=[pltpu.VMEM((features // BLOCK * PAD, quads * BLOCK), jnp.float32)],
        compiler_params=params(),
        name="codes",
    )(where, bucket, sign_bits)


def norm_kernel(pair, turns, where, hidden_ref, gain_ref, *out_refs):
    core, place = where[3], where[4]
    features = out_refs[0].shape[2]
    values = hidden_ref[...].astype(jnp.float32)
    inverse_rms = lax.rsqrt(jnp.mean(values * values, axis=1, keepdims=True) + EPS)
    for other in range(pair):
        for step in range(turns):
            slab = lax.rem(place + step, turns) * pair + (core ^ other)
            span = pl.ds(pl.multiple_of(slab * features, BLOCK), features)
            normed = hidden_ref[:, span].astype(jnp.float32) * inverse_rms
            out_refs[other][step] = (normed * gain_ref[:, span]).astype(jnp.bfloat16)


def norm(where, hidden, gain, pair, turns):
    tokens, width = hidden.shape
    features = width // (pair * turns)
    tile = min(tokens, 32)
    out = jax.ShapeDtypeStruct((turns, tokens, features), jnp.bfloat16)
    return pl.pallas_call(
        functools.partial(norm_kernel, pair, turns),
        out_shape=(out,) * pair,
        grid=(tokens // tile,),
        in_specs=[
            pl.BlockSpec(memory_space=pltpu.SMEM),
            pl.BlockSpec((tile, width), lambda i: (i, 0)),
            pl.BlockSpec((1, width), lambda i: (0, 0)),
        ],
        out_specs=(pl.BlockSpec((turns, tile, features), lambda i: (0, i, 0)),) * pair,
        compiler_params=params(),
        name="normed",
    )(where, hidden, gain)


def sketch_kernel(scale, count, pair, *refs):
    inputs_refs, cot_refs, rows_ref = refs[:pair], refs[pair : 2 * pair], refs[2 * pair]
    table_ref, total = refs[2 * pair + 1 :]
    step = pl.program_id(0)
    contract = (((0,), (0,)), ((), ()))
    inputs = jnp.concatenate([ref[0] for ref in inputs_refs], axis=0)
    cots = jnp.concatenate([ref[...] for ref in cot_refs], axis=0)
    grad = lax.dot_general(inputs, cots, contract, preferred_element_type=jnp.float32) * scale
    quads = rows_ref.shape[0]
    upper = grad.astype(jnp.bfloat16)
    lower = (grad - upper.astype(jnp.float32)).astype(jnp.bfloat16)
    both = jnp.concatenate(
        [
            jnp.concatenate(
                [part[:, quad * BLOCK : (quad + 1) * BLOCK] for part in (upper, lower)], axis=1
            )
            for quad in range(quads)
        ],
        axis=0,
    )
    features = rows_ref.shape[2]
    numbers = lax.broadcasted_iota(jnp.int32, (NBB, features), 0).astype(jnp.bfloat16) + 1

    @pl.when(step == 0)
    def _():
        total[...] = jnp.zeros_like(total)

    for row in range(ROWS):
        picks = []
        for quad in range(quads):
            code = rows_ref[quad, row : row + 1, :]
            sign = jnp.where(code < 0, -1.0, 1.0).astype(jnp.bfloat16)
            picks.append(jnp.where(jnp.abs(code) == numbers, sign, jnp.zeros((), jnp.bfloat16)))
        pick = jnp.concatenate(picks, axis=1)
        total[row] += jnp.dot(pick, both, preferred_element_type=jnp.float32)

    @pl.when(step == pl.num_programs(0) - 1)
    def _():
        share = NBB // count
        for row in range(ROWS):
            table = total[row, :, :BLOCK] + total[row, :, BLOCK:]
            for part in range(count):
                table_ref[part, row] = table[part * share : (part + 1) * share, :].astype(
                    table_ref.dtype
                )


def sketch(inputs, cots, rows, which, scale, count, tile=512):
    tokens, features = inputs[0].shape[1:]
    quads = rows.shape[0]
    tile = min(tile, features)
    pair = len(inputs)
    return pl.pallas_call(
        functools.partial(sketch_kernel, scale, count, pair),
        out_shape=jax.ShapeDtypeStruct((count, ROWS, NBB // count, BLOCK), jnp.bfloat16),
        grid=(features // tile,),
        in_specs=[pl.BlockSpec((1, tokens, tile), lambda i: (which, 0, i))] * pair
        + [pl.BlockSpec(cots[0].shape, lambda i: (0, 0))] * pair
        + [pl.BlockSpec((quads, PAD, tile), lambda i: (0, 0, i))],
        out_specs=pl.BlockSpec((count, ROWS, NBB // count, BLOCK), lambda i: (0, 0, 0, 0)),
        scratch_shapes=[pltpu.VMEM((ROWS, NBB, 2 * BLOCK), jnp.float32)],
        compiler_params=params(),
        name="sketch",
    )(*inputs, *cots, rows)


def grads_kernel(turns, pair, *refs):
    cot_refs, weight_refs, out_refs = refs[:turns], refs[turns : turns + pair], refs[turns + pair :]
    cots = jnp.concatenate([ref[...] for ref in cot_refs], axis=0)
    tokens = cot_refs[0].shape[0]
    for other in range(pair):
        grad = lax.dot_general(
            cots,
            weight_refs[other][...],
            (((1,), (1,)), ((), ())),
            preferred_element_type=jnp.float32,
        ).astype(jnp.bfloat16)
        for step in range(turns):
            out_refs[step][other] = grad[step * tokens : (step + 1) * tokens]


def grads(cots, weights, tile=512):
    turns, pair = len(cots), len(weights)
    tokens, width = cots[0].shape
    features = weights[0].shape[0]
    tile = min(tile, features)
    return pl.pallas_call(
        functools.partial(grads_kernel, turns, pair),
        out_shape=(jax.ShapeDtypeStruct((pair, tokens, features), jnp.bfloat16),) * turns,
        grid=(features // tile,),
        in_specs=[pl.BlockSpec((tokens, width), lambda i: (0, 0))] * turns
        + [pl.BlockSpec((tile, width), lambda i: (i, 0))] * pair,
        out_specs=(pl.BlockSpec((pair, tokens, tile), lambda i: (0, 0, i)),) * turns,
        compiler_params=params(),
        name="input_grad",
    )(*cots, *weights)


def backward_kernel(turns, pair, where, hidden_ref, gain_ref, *refs):
    grad_refs, out_ref = refs[:turns], refs[turns]
    core, place = where[3], where[4]
    features = grad_refs[0].shape[2]
    width = hidden_ref.shape[1]
    values = hidden_ref[...].astype(jnp.float32)
    inverse_rms = lax.rsqrt(jnp.mean(values * values, axis=1, keepdims=True) + EPS)
    spans = []
    total = jnp.zeros((hidden_ref.shape[0], 1), jnp.float32)
    for step in range(turns):
        for other in range(pair):
            slab = lax.rem(place + step, turns) * pair + (core ^ other)
            span = pl.ds(pl.multiple_of(slab * features, BLOCK), features)
            spans.append((step, other, span))
            scaled = grad_refs[step][other].astype(jnp.float32) * gain_ref[:, span]
            normed = hidden_ref[:, span].astype(jnp.float32) * inverse_rms
            total += jnp.sum(scaled * normed, axis=1, keepdims=True)
    mean_term = total / width
    for step, other, span in spans:
        scaled = grad_refs[step][other].astype(jnp.float32) * gain_ref[:, span]
        normed = hidden_ref[:, span].astype(jnp.float32) * inverse_rms
        out_ref[:, span] = (inverse_rms * (scaled - normed * mean_term)).astype(jnp.bfloat16)


def backward(where, hidden, gain, grad_parts):
    tokens, width = hidden.shape
    turns, pair = len(grad_parts), grad_parts[0].shape[0]
    features = grad_parts[0].shape[2]
    tile = min(tokens, 32)
    return pl.pallas_call(
        functools.partial(backward_kernel, turns, pair),
        out_shape=jax.ShapeDtypeStruct((tokens, width), jnp.bfloat16),
        grid=(tokens // tile,),
        in_specs=[
            pl.BlockSpec(memory_space=pltpu.SMEM),
            pl.BlockSpec((tile, width), lambda i: (i, 0)),
            pl.BlockSpec((1, width), lambda i: (0, 0)),
        ]
        + [pl.BlockSpec((pair, tile, features), lambda i: (0, i, 0))] * turns,
        out_specs=pl.BlockSpec((tile, width), lambda i: (i, 0)),
        compiler_params=params(),
        name="hidden_grad",
    )(where, hidden, gain, *grad_parts)


def unsketch_kernel(count, *refs):
    part_refs, cols_ref, rows_ref, error_ref = refs[:count], *refs[count : count + 3]
    update_ref, error_new_ref, total = refs[count + 3 :]
    step = pl.program_id(0)
    quads = rows_ref.shape[0]
    share = NBB // count
    tile = cols_ref.shape[0]
    tables = [jnp.concatenate([ref[row] for ref in part_refs], axis=0) for row in range(ROWS)]
    lanes = (lax.broadcasted_iota(jnp.int32, (tile, NBB), 1) + 1).astype(jnp.float32)
    numbers = lax.broadcasted_iota(jnp.int32, (share, tile), 0).astype(jnp.bfloat16) + 1

    @pl.when(step == 0)
    def _():
        total[...] = jnp.zeros_like(total)

    for quad in range(quads):
        reads = []
        for row in range(ROWS):
            code = cols_ref[:, quad * PAD + row : quad * PAD + row + 1]
            pick = jnp.where(jnp.abs(code) == lanes, 1.0, 0.0).astype(jnp.bfloat16)
            read = jnp.dot(pick, tables[row], preferred_element_type=jnp.float32)
            reads.append(jnp.where(code < 0, -read, read))
        estimate = middle_five(reads)
        update = estimate - jnp.clip(estimate, -THRESHOLD, THRESHOLD)
        update_ref[:, quad * BLOCK : (quad + 1) * BLOCK] = update
        upper = update.astype(jnp.bfloat16)
        lower = (update - upper.astype(jnp.float32)).astype(jnp.bfloat16)
        both = jnp.concatenate([upper, lower], axis=1)
        picks = []
        for row in range(ROWS):
            code = rows_ref[quad, row : row + 1, :]
            sign = jnp.where(code < 0, -1.0, 1.0).astype(jnp.bfloat16)
            picks.append(jnp.where(jnp.abs(code) == numbers, sign, jnp.zeros((), jnp.bfloat16)))
        pick = jnp.concatenate(picks, axis=0)
        total[...] += jnp.dot(pick, both, preferred_element_type=jnp.float32)

    @pl.when(step == pl.num_programs(0) - 1)
    def _():
        for row in range(ROWS):
            rows = slice(row * share, (row + 1) * share)
            error_new_ref[row] = error_ref[row] - (total[rows, :BLOCK] + total[rows, BLOCK:])


def unsketch(parts, cols, rows, error_mid, tile=512):
    count = len(parts)
    features = cols.shape[0]
    quads = rows.shape[0]
    share = NBB // count
    tile = min(tile, features)
    table_spec = pl.BlockSpec((ROWS, share, BLOCK), lambda i: (0, 0, 0))
    return pl.pallas_call(
        functools.partial(unsketch_kernel, count),
        out_shape=(
            jax.ShapeDtypeStruct((features, quads * BLOCK), jnp.float32),
            jax.ShapeDtypeStruct((ROWS, share, BLOCK), jnp.float32),
        ),
        grid=(features // tile,),
        in_specs=[table_spec] * count
        + [
            pl.BlockSpec((tile, quads * PAD), lambda i: (i, 0)),
            pl.BlockSpec((quads, PAD, tile), lambda i: (0, 0, i)),
            table_spec,
        ],
        out_specs=(pl.BlockSpec((tile, quads * BLOCK), lambda i: (i, 0)), table_spec),
        scratch_shapes=[pltpu.VMEM((ROWS * share, 2 * BLOCK), jnp.float32)],
        compiler_params=params(),
        name="unsketch",
    )(*parts, cols, rows, error_mid)


def on_device(hidden_states, gain, key_weight, key_cotangent, bucket, sign_bits, momentum, error):
    fsdp_count = lax.axis_size("fsdp")
    dp_count = lax.axis_size("dp")
    pair = 2 if fsdp_count % 2 == 0 else 1
    turns = fsdp_count // pair
    tokens, width = hidden_states.shape
    quads = key_cotangent.shape[1] // BLOCK
    share = NBB // dp_count
    scale = 1.0 / math.sqrt(tokens * fsdp_count)
    dp_at, fsdp_at = lax.axis_index("dp"), lax.axis_index("fsdp")
    core, place = fsdp_at % pair, fsdp_at // pair
    power = 1 if dp_count & (dp_count - 1) == 0 else 0
    where = jnp.stack([jnp.int32(0), dp_at * share, jnp.int32(power), core, place]).astype(jnp.int32)
    gain = gain.reshape(1, width)

    def across(value):
        return lax.ppermute(value, "fsdp", [(i, i ^ 1) for i in range(fsdp_count)])

    def from_turn(value, step):
        pairs = [
            (((i // pair + step) % turns) * pair + i % pair, i) for i in range(fsdp_count)
        ]
        return lax.ppermute(value, "fsdp", pairs)

    def to_turn(value, step):
        return from_turn(value, turns - step)

    def to_share(value, step):
        return lax.ppermute(value, "dp", [(i, partner(i, step, dp_count)) for i in range(dp_count)])

    def from_share(value, step):
        return lax.ppermute(value, "dp", [(partner(i, step, dp_count), i) for i in range(dp_count)])

    rows, cols = prep(where, bucket, sign_bits, quads)
    rows_at = [rows] + [from_turn(rows, step) for step in range(1, turns)]
    inputs = list(norm(where, hidden_states, gain, pair, turns))
    cots = [key_cotangent]
    if pair == 2:
        inputs[1] = across(inputs[1])
        cots.append(across(key_cotangent))
    received = []
    for step in range(1, turns):
        table = sketch(inputs, cots, rows_at[step], step, scale, dp_count)
        received.append(to_turn(table, step))
    table = sketch(inputs, cots, rows, 0, scale, dp_count).astype(jnp.float32)
    for other in received:
        table = table + other.astype(jnp.float32)

    weights = [key_weight] + ([across(key_weight)] if pair == 2 else [])
    turn_cots = [key_cotangent] + [from_turn(key_cotangent, step) for step in range(1, turns)]
    grad_parts = grads(turn_cots, weights)
    grad_parts = [grad_parts[0]] + [
        from_turn(grad_parts[turns - step], step) for step in range(1, turns)
    ]
    hidden_grad = backward(where, hidden_states, gain, grad_parts)

    sent = table.astype(jnp.bfloat16)
    total = table[0]
    order = sorted(range(1, dp_count), key=lambda step: -bin(step).count("1") * 100 - step)
    arrived = [to_share(sent[step], step) for step in order]
    for part in arrived:
        total = total + part.astype(jnp.float32)
    momentum_new = DECAY * momentum.reshape(ROWS, share, BLOCK) + total / dp_count
    error_mid = error.reshape(ROWS, share, BLOCK) + momentum_new
    error_sent = error_mid.astype(jnp.bfloat16)
    gathered = {step: from_share(error_sent, step) for step in order}
    parts = [error_sent] + [gathered[step] for step in range(1, dp_count)]
    update, error_new = unsketch(parts, cols, rows, error_mid)
    return (
        hidden_grad,
        momentum_new.reshape(momentum.shape),
        error_new.reshape(error.shape),
        update,
    )


def solution(mesh):
    in_specs = (
        P(("dp", "fsdp"), None),
        P(),
        P("fsdp", None),
        P(("dp", "fsdp"), None),
        P(None, "fsdp"),
        P(None, "fsdp"),
        P("fsdp", None, "dp"),
        P("fsdp", None, "dp"),
    )
    out_specs = (
        P(("dp", "fsdp"), None),
        P("fsdp", None, "dp"),
        P("fsdp", None, "dp"),
        P("fsdp", None),
    )
    return jax.shard_map(
        on_device, mesh=mesh, in_specs=in_specs, out_specs=out_specs, check_vma=False
    )
```

```python
import functools
import math

import jax
import jax.numpy as jnp
from jax import lax
from jax.experimental import pallas as pl
from jax.experimental.pallas import tpu as pltpu
from jax.sharding import PartitionSpec as P

ROWS = 5
NBB = 256
BLOCK = 128
PAD = 8

EPS = 1e-05
DECAY = 0.9
THRESHOLD = 1.0
MIB = 1024 * 1024
SMALL = pl.CostEstimate(flops=1, bytes_accessed=1, transcendentals=0)


def params(limit=48):
    return pltpu.CompilerParams(vmem_limit_bytes=limit * MIB)


def middle_three(first, second, third):
    return jnp.maximum(jnp.minimum(first, second), jnp.minimum(jnp.maximum(first, second), third))


def middle_five(items):
    upper_pair = jnp.minimum(jnp.maximum(items[0], items[1]), jnp.maximum(items[2], items[3]))
    lower_pair = jnp.maximum(jnp.minimum(items[0], items[1]), jnp.minimum(items[2], items[3]))
    return middle_three(items[4], upper_pair, lower_pair)


def picked(code, numbers):
    sign = jnp.where(code < 0, -1.0, 1.0).astype(jnp.bfloat16)
    return jnp.where(jnp.abs(code) == numbers, sign, jnp.zeros((), jnp.bfloat16))


def partner(index, step, count):
    if count & (count - 1) == 0:
        return index ^ step
    return (index + step) % count


def codes(wrap, bucket_ref, sign_ref, rows_ref, stacked):
    share = lax.axis_index("dp") * (NBB // lax.axis_size("dp"))
    quads = rows_ref.shape[0]
    width = quads * BLOCK
    groups = bucket_ref.shape[1] // width
    bucket = bucket_ref[...]
    bucket = lax.rem(bucket + (NBB - share), NBB) if wrap else bucket ^ share
    code = ((bucket + 1) * (2 * sign_ref[...] - 1)).astype(jnp.float32)
    stacked[...] = jnp.zeros_like(stacked)
    for group in range(groups):
        stacked[group * PAD : group * PAD + ROWS, :] = code[:, group * width : (group + 1) * width]
    source = lax.broadcasted_iota(jnp.int32, (width, width), 0)
    target = lax.broadcasted_iota(jnp.int32, (width, width), 1)
    chosen = source == quads * (target % BLOCK) + target // BLOCK
    order = jnp.where(chosen, 1.0, 0.0).astype(jnp.bfloat16)
    moved = jnp.dot(stacked[...].astype(jnp.bfloat16), order, preferred_element_type=jnp.float32)
    for group in range(groups):
        for quad in range(quads):
            rows_ref[quad, :, group * BLOCK : (group + 1) * BLOCK] = moved[
                group * PAD : (group + 1) * PAD, quad * BLOCK : (quad + 1) * BLOCK
            ].astype(rows_ref.dtype)


def front_kernel(wrap, pair, turns, bucket_ref, sign_ref, hidden_ref, gain_ref, *refs):
    rows_ref, out_refs, stacked = refs[0], refs[1 : 1 + pair], refs[1 + pair]

    @pl.when(pl.program_id(0) == 0)
    def _():
        codes(wrap, bucket_ref, sign_ref, rows_ref, stacked)

    fsdp_at = lax.axis_index("fsdp")
    core, place = lax.rem(fsdp_at, pair), fsdp_at // pair
    features = out_refs[0].shape[2]
    values = hidden_ref[...].astype(jnp.float32)
    inverse_rms = lax.rsqrt(jnp.mean(values * values, axis=1, keepdims=True) + EPS)
    for other in range(pair):
        for step in range(turns):
            slab = lax.rem(place + step, turns) * pair + (core ^ other)
            span = pl.ds(pl.multiple_of(slab * features, BLOCK), features)
            normed = hidden_ref[:, span].astype(jnp.float32) * inverse_rms
            out_refs[other][step] = (normed * gain_ref[:, span]).astype(jnp.bfloat16)


def front(bucket, sign_bits, hidden, gain, quads, wrap, pair, turns, tile=64):
    tokens, width = hidden.shape
    features = width // (pair * turns)
    tile = min(tokens, tile)
    out = jax.ShapeDtypeStruct((turns, tokens, features), jnp.bfloat16)
    return pl.pallas_call(
        functools.partial(front_kernel, wrap, pair, turns),
        out_shape=(jax.ShapeDtypeStruct((quads, PAD, features), jnp.bfloat16),) + (out,) * pair,
        grid=(tokens // tile,),
        in_specs=[
            pl.BlockSpec(bucket.shape, lambda i: (0, 0)),
            pl.BlockSpec(bucket.shape, lambda i: (0, 0)),
            pl.BlockSpec((tile, width), lambda i: (i, 0)),
            pl.BlockSpec((1, width), lambda i: (0, 0)),
        ],
        out_specs=(pl.BlockSpec((quads, PAD, features), lambda i: (0, 0, 0)),)
        + (pl.BlockSpec((turns, tile, features), lambda i: (0, i, 0)),) * pair,
        scratch_shapes=[pltpu.VMEM((features // BLOCK * PAD, quads * BLOCK), jnp.float32)],
        compiler_params=params(60),
        cost_estimate=SMALL,
        name="codes_and_normed",
    )(bucket, sign_bits, hidden, gain)


def sketch_kernel(scale, count, pair, *refs):
    inputs_refs, cot_refs, rows_ref = refs[:pair], refs[pair : 2 * pair], refs[2 * pair]
    table_ref, total = refs[2 * pair + 1 :]
    step = pl.program_id(0)
    contract = (((0,), (0,)), ((), ()))
    inputs = jnp.concatenate([ref[0] for ref in inputs_refs], axis=0)
    cots = jnp.concatenate([ref[...] for ref in cot_refs], axis=0)
    grad = lax.dot_general(inputs, cots, contract, preferred_element_type=jnp.float32) * scale
    quads = rows_ref.shape[0]
    upper = grad.astype(jnp.bfloat16)
    lower = (grad - upper.astype(jnp.float32)).astype(jnp.bfloat16)
    both = jnp.concatenate(
        [
            jnp.concatenate(
                [part[:, quad * BLOCK : (quad + 1) * BLOCK] for part in (upper, lower)], axis=1
            )
            for quad in range(quads)
        ],
        axis=0,
    )
    features = rows_ref.shape[2]
    numbers = lax.broadcasted_iota(jnp.int32, (NBB, features), 0).astype(jnp.bfloat16) + 1

    @pl.when(step == 0)
    def _():
        total[...] = jnp.zeros_like(total)

    for row in range(ROWS):
        picks = []
        for quad in range(quads):
            picks.append(picked(rows_ref[quad, row : row + 1, :], numbers))
        pick = jnp.concatenate(picks, axis=1)
        total[row] += jnp.dot(pick, both, preferred_element_type=jnp.float32)

    @pl.when(step == pl.num_programs(0) - 1)
    def _():
        share = NBB // count
        for row in range(ROWS):
            table = total[row, :, :BLOCK] + total[row, :, BLOCK:]
            for part in range(count):
                table_ref[part, row] = table[part * share : (part + 1) * share, :].astype(
                    table_ref.dtype
                )


def sketch(inputs, cots, rows, which, scale, count, tile=2048):
    tokens, features = inputs[0].shape[1:]
    quads = rows.shape[0]
    tile = min(tile, features)
    pair = len(inputs)
    return pl.pallas_call(
        functools.partial(sketch_kernel, scale, count, pair),
        out_shape=jax.ShapeDtypeStruct((count, ROWS, NBB // count, BLOCK), jnp.bfloat16),
        grid=(features // tile,),
        in_specs=[pl.BlockSpec((1, tokens, tile), lambda i: (which, 0, i))] * pair
        + [pl.BlockSpec(cots[0].shape, lambda i: (0, 0))] * pair
        + [pl.BlockSpec((quads, PAD, tile), lambda i: (0, 0, i))],
        out_specs=pl.BlockSpec((count, ROWS, NBB // count, BLOCK), lambda i: (0, 0, 0, 0)),
        scratch_shapes=[pltpu.VMEM((ROWS, NBB, 2 * BLOCK), jnp.float32)],
        compiler_params=params(),
        cost_estimate=SMALL,
        name="sketch",
    )(*inputs, *cots, rows)


def grads_kernel(turns, pair, *refs):
    cot_refs, weight_refs, out_refs = refs[:turns], refs[turns : turns + pair], refs[turns + pair :]
    cots = jnp.concatenate([ref[...] for ref in cot_refs], axis=0)
    tokens = cot_refs[0].shape[0]
    for other in range(pair):
        grad = lax.dot_general(
            cots,
            weight_refs[other][...],
            (((1,), (1,)), ((), ())),
            preferred_element_type=jnp.float32,
        ).astype(jnp.bfloat16)
        for step in range(turns):
            out_refs[step][other] = grad[step * tokens : (step + 1) * tokens]


def grads(cots, weights, tile=1024):
    turns, pair = len(cots), len(weights)
    tokens, width = cots[0].shape
    features = weights[0].shape[0]
    tile = min(tile, features)
    return pl.pallas_call(
        functools.partial(grads_kernel, turns, pair),
        out_shape=(jax.ShapeDtypeStruct((pair, tokens, features), jnp.bfloat16),) * turns,
        grid=(features // tile,),
        in_specs=[pl.BlockSpec((tokens, width), lambda i: (0, 0))] * turns
        + [pl.BlockSpec((tile, width), lambda i: (i, 0))] * pair,
        out_specs=(pl.BlockSpec((pair, tokens, tile), lambda i: (0, 0, i)),) * turns,
        compiler_params=params(),
        cost_estimate=SMALL,
        name="input_grad",
    )(*cots, *weights)


def backward_kernel(turns, pair, hidden_ref, gain_ref, *refs):
    grad_refs, out_ref = refs[:turns], refs[turns]
    fsdp_at = lax.axis_index("fsdp")
    core, place = lax.rem(fsdp_at, pair), fsdp_at // pair
    features = grad_refs[0].shape[2]
    width = hidden_ref.shape[1]
    values = hidden_ref[...].astype(jnp.float32)
    inverse_rms = lax.rsqrt(jnp.mean(values * values, axis=1, keepdims=True) + EPS)
    spans = []
    total = jnp.zeros((hidden_ref.shape[0], 1), jnp.float32)
    for step in range(turns):
        for other in range(pair):
            slab = lax.rem(place + step, turns) * pair + (core ^ other)
            span = pl.ds(pl.multiple_of(slab * features, BLOCK), features)
            spans.append((step, other, span))
            scaled = grad_refs[step][other].astype(jnp.float32) * gain_ref[:, span]
            normed = hidden_ref[:, span].astype(jnp.float32) * inverse_rms
            total += jnp.sum(scaled * normed, axis=1, keepdims=True)
    mean_term = total / width
    for step, other, span in spans:
        scaled = grad_refs[step][other].astype(jnp.float32) * gain_ref[:, span]
        normed = hidden_ref[:, span].astype(jnp.float32) * inverse_rms
        out_ref[:, span] = (inverse_rms * (scaled - normed * mean_term)).astype(jnp.bfloat16)


def backward(hidden, gain, grad_parts):
    tokens, width = hidden.shape
    turns, pair = len(grad_parts), grad_parts[0].shape[0]
    features = grad_parts[0].shape[2]
    tile = min(tokens, 64)
    return pl.pallas_call(
        functools.partial(backward_kernel, turns, pair),
        out_shape=jax.ShapeDtypeStruct((tokens, width), jnp.bfloat16),
        grid=(tokens // tile,),
        in_specs=[
            pl.BlockSpec((tile, width), lambda i: (i, 0)),
            pl.BlockSpec((1, width), lambda i: (0, 0)),
        ]
        + [pl.BlockSpec((pair, tile, features), lambda i: (0, i, 0))] * turns,
        out_specs=pl.BlockSpec((tile, width), lambda i: (i, 0)),
        compiler_params=params(),
        cost_estimate=SMALL,
        name="hidden_grad",
    )(hidden, gain, *grad_parts)


def unsketch_kernel(count, *refs):
    part_refs, rows_ref, error_ref = refs[:count], *refs[count : count + 2]
    update_ref, error_new_ref, total, tables = refs[count + 2 :]
    step = pl.program_id(0)
    quads, tile = rows_ref.shape[0], rows_ref.shape[2]
    share = NBB // count
    numbers = lax.broadcasted_iota(jnp.int32, (NBB, tile), 0).astype(jnp.bfloat16) + 1

    @pl.when(step == 0)
    def _():
        total[...] = jnp.zeros_like(total)
        for row in range(ROWS):
            table = jnp.concatenate([ref[row] for ref in part_refs], axis=0)
            tables[row] = table.astype(jnp.float32).T.astype(jnp.bfloat16)

    for quad in range(quads):
        reads, own = [], []
        for row in range(ROWS):
            pick = picked(rows_ref[quad, row : row + 1, :], numbers)
            own.append(pick[:share])
            reads.append(jnp.dot(tables[row], pick, preferred_element_type=jnp.float32))
        estimate = middle_five(reads)
        update = (estimate - jnp.clip(estimate, -THRESHOLD, THRESHOLD)).T
        update_ref[:, quad * BLOCK : (quad + 1) * BLOCK] = update
        upper = update.astype(jnp.bfloat16)
        lower = (update - upper.astype(jnp.float32)).astype(jnp.bfloat16)
        both = jnp.concatenate([upper, lower], axis=1)
        total[...] += jnp.dot(
            jnp.concatenate(own, axis=0), both, preferred_element_type=jnp.float32
        )

    @pl.when(step == pl.num_programs(0) - 1)
    def _():
        for row in range(ROWS):
            rows = slice(row * share, (row + 1) * share)
            error_new_ref[row] = error_ref[row] - (total[rows, :BLOCK] + total[rows, BLOCK:])


def unsketch(parts, rows, error_mid, tile=1024):
    count = len(parts)
    quads, _, features = rows.shape
    share = NBB // count
    tile = min(tile, features)
    table_spec = pl.BlockSpec((ROWS, share, BLOCK), lambda i: (0, 0, 0))
    return pl.pallas_call(
        functools.partial(unsketch_kernel, count),
        out_shape=(
            jax.ShapeDtypeStruct((features, quads * BLOCK), jnp.float32),
            jax.ShapeDtypeStruct((ROWS, share, BLOCK), jnp.float32),
        ),
        grid=(features // tile,),
        in_specs=[table_spec] * count
        + [pl.BlockSpec((quads, PAD, tile), lambda i: (0, 0, i)), table_spec],
        out_specs=(pl.BlockSpec((tile, quads * BLOCK), lambda i: (i, 0)), table_spec),
        scratch_shapes=[
            pltpu.VMEM((ROWS * share, 2 * BLOCK), jnp.float32),
            pltpu.VMEM((ROWS, BLOCK, NBB), jnp.bfloat16),
        ],
        compiler_params=params(),
        cost_estimate=SMALL,
        name="unsketch",
    )(*parts, rows, error_mid)


def on_device(hidden_states, gain, key_weight, key_cotangent, bucket, sign_bits, momentum, error):
    fsdp_count = lax.axis_size("fsdp")
    dp_count = lax.axis_size("dp")
    pair = 2 if fsdp_count % 2 == 0 else 1
    turns = fsdp_count // pair
    tokens, width = hidden_states.shape
    quads = key_cotangent.shape[1] // BLOCK
    share = NBB // dp_count
    scale = 1.0 / math.sqrt(tokens * fsdp_count)
    wrap = dp_count & (dp_count - 1) != 0
    gain = gain.reshape(1, width)

    def across(value):
        return lax.ppermute(value, "fsdp", [(i, i ^ 1) for i in range(fsdp_count)])

    def from_turn(value, step):
        pairs = [
            (((i // pair + step) % turns) * pair + i % pair, i) for i in range(fsdp_count)
        ]
        return lax.ppermute(value, "fsdp", pairs)

    def to_turn(value, step):
        return from_turn(value, turns - step)

    def to_share(value, step):
        return lax.ppermute(value, "dp", [(i, partner(i, step, dp_count)) for i in range(dp_count)])

    def from_share(value, step):
        return lax.ppermute(value, "dp", [(partner(i, step, dp_count), i) for i in range(dp_count)])

    weights = [key_weight] + ([across(key_weight)] if pair == 2 else [])
    turn_cots = [key_cotangent] + [from_turn(key_cotangent, step) for step in range(1, turns)]
    cots = [key_cotangent] + ([across(key_cotangent)] if pair == 2 else [])
    rows, *inputs = front(
        bucket, sign_bits, hidden_states, gain, quads, wrap, pair, turns
    )
    rows, inputs, turn_cots = lax.optimization_barrier((rows, inputs, turn_cots))
    rows_at = [rows] + [from_turn(rows, step) for step in range(1, turns)]
    if pair == 2:
        inputs[1] = across(inputs[1])
    grad_parts = grads(turn_cots, weights)
    rows_at, grad_parts = lax.optimization_barrier((rows_at, grad_parts))
    received = []
    for step in range(1, turns):
        table = sketch(inputs, cots, rows_at[step], step, scale, dp_count)
        received.append(to_turn(table, step))
    table = sketch(inputs, cots, rows, 0, scale, dp_count).astype(jnp.float32)
    grad_parts = [grad_parts[0]] + [
        from_turn(grad_parts[turns - step], step) for step in range(1, turns)
    ]
    hidden_grad = backward(hidden_states, gain, grad_parts)

    for other in received:
        table = table + other.astype(jnp.float32)
    sent = table.astype(jnp.bfloat16)
    total = table[0]
    order = sorted(range(1, dp_count), key=lambda step: -bin(step).count("1") * 100 - step)
    arrived = [to_share(sent[step], step) for step in range(1, dp_count)]
    for part in arrived:
        total = total + part.astype(jnp.float32)
    momentum_new = DECAY * momentum.reshape(ROWS, share, BLOCK) + total / dp_count
    error_mid = error.reshape(ROWS, share, BLOCK) + momentum_new
    error_sent = error_mid.astype(jnp.bfloat16)
    gathered = {step: from_share(error_sent, step) for step in order}
    parts = [error_sent] + [gathered[step] for step in range(1, dp_count)]
    parts, hidden_grad = lax.optimization_barrier((parts, hidden_grad))
    update, error_new = unsketch(parts, rows, error_mid)
    return (
        hidden_grad,
        momentum_new.reshape(momentum.shape),
        error_new.reshape(error.shape),
        update,
    )


def solution(mesh):
    in_specs = (
        P(("dp", "fsdp"), None),
        P(),
        P("fsdp", None),
        P(("dp", "fsdp"), None),
        P(None, "fsdp"),
        P(None, "fsdp"),
        P("fsdp", None, "dp"),
        P("fsdp", None, "dp"),
    )
    out_specs = (
        P(("dp", "fsdp"), None),
        P("fsdp", None, "dp"),
        P("fsdp", None, "dp"),
        P("fsdp", None),
    )
    return jax.shard_map(
        on_device, mesh=mesh, in_specs=in_specs, out_specs=out_specs, check_vma=False
    )
```

```python
import functools
import math

import jax
import jax.numpy as jnp
from jax import lax
from jax.experimental import pallas as pl
from jax.experimental.pallas import tpu as pltpu
from jax.sharding import PartitionSpec as P

ROWS = 5
NBB = 256
BLOCK = 128
PAD = 8

EPS = 1e-05
DECAY = 0.9
THRESHOLD = 1.0
MIB = 1024 * 1024
HALVES = 2
SMALL = pl.CostEstimate(flops=1, bytes_accessed=1, transcendentals=0)


def params(limit=48):
    return pltpu.CompilerParams(vmem_limit_bytes=limit * MIB)


def middle_three(first, second, third):
    return jnp.maximum(jnp.minimum(first, second), jnp.minimum(jnp.maximum(first, second), third))


def middle_five(items):
    upper_pair = jnp.minimum(jnp.maximum(items[0], items[1]), jnp.maximum(items[2], items[3]))
    lower_pair = jnp.maximum(jnp.minimum(items[0], items[1]), jnp.minimum(items[2], items[3]))
    return middle_three(items[4], upper_pair, lower_pair)


def picked(code, numbers):
    sign = jnp.where(code < 0, -1.0, 1.0).astype(jnp.bfloat16)
    return jnp.where(jnp.abs(code) == numbers, sign, jnp.zeros((), jnp.bfloat16))


def partner(index, step, count):
    if count & (count - 1) == 0:
        return index ^ step
    return (index + step) % count


def codes(wrap, bucket_ref, sign_ref, rows_ref, packed_ref, stacked, packed):
    share = lax.axis_index("dp") * (NBB // lax.axis_size("dp"))
    quads = rows_ref.shape[0]
    width = quads * BLOCK
    groups = bucket_ref.shape[1] // width
    bucket = bucket_ref[...]
    bucket = lax.rem(bucket + (NBB - share), NBB) if wrap else bucket ^ share
    code = ((bucket + 1) * (2 * sign_ref[...] - 1)).astype(jnp.float32)
    stacked[...] = jnp.zeros_like(stacked)
    for group in range(groups):
        stacked[group * PAD : group * PAD + ROWS, :] = code[:, group * width : (group + 1) * width]
    source = lax.broadcasted_iota(jnp.int32, (width, width), 0)
    target = lax.broadcasted_iota(jnp.int32, (width, width), 1)
    chosen = source == quads * (target % BLOCK) + target // BLOCK
    order = jnp.where(chosen, 1.0, 0.0).astype(jnp.bfloat16)
    moved = jnp.dot(stacked[...].astype(jnp.bfloat16), order, preferred_element_type=jnp.float32)
    for group in range(groups):
        for quad in range(quads):
            part = moved[group * PAD : (group + 1) * PAD, quad * BLOCK : (quad + 1) * BLOCK]
            rows_ref[quad, :, group * BLOCK : (group + 1) * BLOCK] = part.astype(rows_ref.dtype)
            half, place = divmod(group, groups // HALVES)
            first = (quad * HALVES + half) * ROWS
            packed[first : first + ROWS, place * BLOCK : (place + 1) * BLOCK] = part[:ROWS]
    packed_ref[...] = packed[...].astype(packed_ref.dtype)


def front_kernel(wrap, pair, turns, bucket_ref, sign_ref, hidden_ref, gain_ref, *refs):
    rows_ref, packed_ref, out_refs = refs[0], refs[1], refs[2 : 2 + pair]

    @pl.when(pl.program_id(0) == 0)
    def _():
        codes(wrap, bucket_ref, sign_ref, rows_ref, packed_ref, *refs[2 + pair :])

    fsdp_at = lax.axis_index("fsdp")
    core, place = lax.rem(fsdp_at, pair), fsdp_at // pair
    features = out_refs[0].shape[2]
    values = hidden_ref[...].astype(jnp.float32)
    inverse_rms = lax.rsqrt(jnp.mean(values * values, axis=1, keepdims=True) + EPS)
    for other in range(pair):
        for step in range(turns):
            slab = lax.rem(place + step, turns) * pair + (core ^ other)
            span = pl.ds(pl.multiple_of(slab * features, BLOCK), features)
            normed = hidden_ref[:, span].astype(jnp.float32) * inverse_rms
            out_refs[other][step] = (normed * gain_ref[:, span]).astype(jnp.bfloat16)


def front(bucket, sign_bits, hidden, gain, quads, wrap, pair, turns, tile=64):
    tokens, width = hidden.shape
    features = width // (pair * turns)
    tile = min(tokens, tile)
    out = jax.ShapeDtypeStruct((turns, tokens, features), jnp.bfloat16)
    packed = (quads * HALVES * ROWS, features // HALVES)
    return pl.pallas_call(
        functools.partial(front_kernel, wrap, pair, turns),
        out_shape=(
            jax.ShapeDtypeStruct((quads, PAD, features), jnp.bfloat16),
            jax.ShapeDtypeStruct(packed, jnp.bfloat16),
        )
        + (out,) * pair,
        grid=(tokens // tile,),
        in_specs=[
            pl.BlockSpec(bucket.shape, lambda i: (0, 0)),
            pl.BlockSpec(bucket.shape, lambda i: (0, 0)),
            pl.BlockSpec((tile, width), lambda i: (i, 0)),
            pl.BlockSpec((1, width), lambda i: (0, 0)),
        ],
        out_specs=(
            pl.BlockSpec((quads, PAD, features), lambda i: (0, 0, 0)),
            pl.BlockSpec(packed, lambda i: (0, 0)),
        )
        + (pl.BlockSpec((turns, tile, features), lambda i: (0, i, 0)),) * pair,
        scratch_shapes=[
            pltpu.VMEM((features // BLOCK * PAD, quads * BLOCK), jnp.float32),
            pltpu.VMEM(packed, jnp.float32),
        ],
        compiler_params=params(60),
        cost_estimate=SMALL,
        name="codes_and_normed",
    )(bucket, sign_bits, hidden, gain)


def sketch_kernel(scale, count, near, pair, quads, *refs):
    inputs_refs, cot_refs, rows_ref = refs[:pair], refs[pair : 2 * pair], refs[2 * pair]
    table_ref = refs[2 * pair + 1]
    contract = (((0,), (0,)), ((), ()))
    inputs = jnp.concatenate([ref[0] for ref in inputs_refs], axis=0)
    cots = jnp.concatenate([ref[...] for ref in cot_refs], axis=0)
    grad = lax.dot_general(inputs, cots, contract, preferred_element_type=jnp.float32) * scale
    upper = grad.astype(jnp.bfloat16)
    lower = (grad - upper.astype(jnp.float32)).astype(jnp.bfloat16)
    both = jnp.concatenate(
        [
            jnp.concatenate(
                [part[:, quad * BLOCK : (quad + 1) * BLOCK] for part in (upper, lower)], axis=1
            )
            for quad in range(quads)
        ],
        axis=0,
    )
    features = inputs.shape[1]
    pieces = 1 if len(rows_ref.shape) == 3 else HALVES
    numbers = lax.broadcasted_iota(jnp.int32, (NBB, features // pieces), 0)
    numbers = numbers.astype(jnp.bfloat16) + 1
    share = NBB // count
    for row in range(ROWS):
        picks = []
        for quad in range(quads):
            for piece in range(pieces):
                if pieces == 1:
                    code = rows_ref[quad, row : row + 1, :]
                else:
                    at = (quad * HALVES + piece) * ROWS + row
                    code = rows_ref[at : at + 1, :]
                picks.append(picked(code, numbers))
        pick = jnp.concatenate(picks, axis=1)
        sums = jnp.dot(pick, both, preferred_element_type=jnp.float32)
        table = sums[:, :BLOCK] + sums[:, BLOCK:]
        for part in range(count):
            table_ref[part % near * (count // near) + part // near, row] = table[part * share : (part + 1) * share, :].astype(
                table_ref.dtype
            )


def sketch(inputs, cots, rows, which, scale, count, near):
    tokens, features = inputs[0].shape[1:]
    quads = cots[0].shape[1] // BLOCK
    pair = len(inputs)
    table = (count, ROWS, NBB // count, BLOCK)
    return pl.pallas_call(
        functools.partial(sketch_kernel, scale, count, near, pair, quads),
        out_shape=jax.ShapeDtypeStruct(table, jnp.bfloat16),
        grid=(1,),
        in_specs=[pl.BlockSpec((1, tokens, features), lambda i: (which, 0, 0))] * pair
        + [pl.BlockSpec(cots[0].shape, lambda i: (0, 0))] * pair
        + [pl.BlockSpec(rows.shape, lambda i: (0,) * rows.ndim)],
        out_specs=pl.BlockSpec(table, lambda i: (0, 0, 0, 0)),
        compiler_params=params(),
        cost_estimate=pl.CostEstimate(
            flops=4 * ROWS * NBB * quads * features * BLOCK,
            bytes_accessed=4 * pair * tokens * features,
            transcendentals=0,
        ),
        name="sketch",
    )(*inputs, *cots, rows)


def grads_kernel(turns, *refs):
    cot_refs, weight_refs, out_refs = refs[:turns], refs[turns:-turns], refs[-turns:]
    cots = jnp.concatenate([ref[...] for ref in cot_refs], axis=0)
    tokens = cot_refs[0].shape[0]
    for index, weight_ref in enumerate(weight_refs):
        grad = lax.dot_general(
            cots, weight_ref[...], (((1,), (1,)), ((), ())), preferred_element_type=jnp.float32
        ).astype(jnp.bfloat16)
        for step in range(turns):
            out_refs[step][index] = grad[step * tokens : (step + 1) * tokens]


def grads(cots, weights, pieces):
    turns = len(cots)
    tokens, width = cots[0].shape
    size = weights[0].shape[0] // HALVES
    out = (len(pieces), tokens, size)
    return pl.pallas_call(
        functools.partial(grads_kernel, turns),
        out_shape=(jax.ShapeDtypeStruct(out, jnp.bfloat16),) * turns,
        grid=(1,),
        in_specs=[pl.BlockSpec((tokens, width), lambda i: (0, 0))] * turns
        + [
            pl.BlockSpec((size, width), functools.partial(lambda half, i: (half, 0), half))
            for _, half in pieces
        ],
        out_specs=(pl.BlockSpec(out, lambda i: (0, 0, 0)),) * turns,
        compiler_params=params(),
        cost_estimate=SMALL,
        name="input_grad",
    )(*cots, *[weights[other] for other, _ in pieces])


def backward_kernel(turns, pair, pieces, hidden_ref, gain_ref, *refs):
    grad_refs, out_ref = refs[:-1], refs[-1]
    fsdp_at = lax.axis_index("fsdp")
    core, place = lax.rem(fsdp_at, pair), fsdp_at // pair
    width = hidden_ref.shape[1]
    features = width // (turns * pair)
    size = features // HALVES
    spans = []
    squares = jnp.zeros((hidden_ref.shape[0], BLOCK), jnp.float32)
    products = squares
    for (step, halves), grad_ref in zip(pieces, grad_refs):
        for index, (other, half) in enumerate(halves):
            slab = lax.rem(place + step, turns) * pair + (core ^ other)
            start = slab * features + half * size
            for part in range(0, size, BLOCK):
                span = pl.ds(pl.multiple_of(start + part, BLOCK), BLOCK)
                values = hidden_ref[:, span].astype(jnp.float32)
                grad = grad_ref[index, :, part : part + BLOCK].astype(jnp.float32)
                squares += values * values
                products += grad * gain_ref[:, span] * values
            spans.append((grad_ref, index, pl.ds(pl.multiple_of(start, BLOCK), size)))
    inverse_rms = lax.rsqrt(jnp.sum(squares, axis=1, keepdims=True) / width + EPS)
    mean_term = inverse_rms * jnp.sum(products, axis=1, keepdims=True) / width
    shrink = inverse_rms * (inverse_rms * mean_term)
    for grad_ref, index, span in spans:
        scaled = grad_ref[index].astype(jnp.float32) * gain_ref[:, span]
        values = hidden_ref[:, span].astype(jnp.float32)
        out_ref[:, span] = (inverse_rms * scaled - shrink * values).astype(jnp.bfloat16)


def backward(hidden, gain, grad_parts, pieces, turns, pair, tile=32):
    tokens, width = hidden.shape
    tile = min(tokens, tile)
    return pl.pallas_call(
        functools.partial(backward_kernel, turns, pair, pieces),
        out_shape=jax.ShapeDtypeStruct((tokens, width), jnp.bfloat16),
        grid=(tokens // tile,),
        in_specs=[
            pl.BlockSpec((tile, width), lambda i: (i, 0)),
            pl.BlockSpec((1, width), lambda i: (0, 0)),
        ]
        + [
            pl.BlockSpec((part.shape[0], tile, part.shape[2]), lambda i: (0, i, 0))
            for part in grad_parts
        ],
        out_specs=pl.BlockSpec((tile, width), lambda i: (i, 0)),
        compiler_params=params(),
        cost_estimate=SMALL,
        name="hidden_grad",
    )(hidden, gain, *grad_parts)


def unsketch_kernel(groups, share, *refs):
    part_refs, rows_ref, error_ref = refs[:groups], *refs[groups : groups + 2]
    update_ref, error_new_ref, total, tables = refs[groups + 2 :]
    step = pl.program_id(0)
    quads, tile = rows_ref.shape[0], rows_ref.shape[2]
    numbers = lax.broadcasted_iota(jnp.int32, (NBB, tile), 0).astype(jnp.bfloat16) + 1

    @pl.when(step == 0)
    def _():
        total[...] = jnp.zeros_like(total)
        for row in range(ROWS):
            table = jnp.concatenate(
                [ref[near, row] for ref in part_refs for near in range(ref.shape[0])], axis=0
            )
            tables[row] = table.astype(jnp.float32).T.astype(jnp.bfloat16)

    for quad in range(quads):
        reads, own = [], []
        for row in range(ROWS):
            pick = picked(rows_ref[quad, row : row + 1, :], numbers)
            own.append(pick[:share])
            reads.append(jnp.dot(tables[row], pick, preferred_element_type=jnp.float32))
        estimate = middle_five(reads)
        update = (estimate - jnp.clip(estimate, -THRESHOLD, THRESHOLD)).T
        update_ref[:, quad * BLOCK : (quad + 1) * BLOCK] = update
        upper = update.astype(jnp.bfloat16)
        lower = (update - upper.astype(jnp.float32)).astype(jnp.bfloat16)
        both = jnp.concatenate([upper, lower], axis=1)
        total[...] += jnp.dot(
            jnp.concatenate(own, axis=0), both, preferred_element_type=jnp.float32
        )

    @pl.when(step == pl.num_programs(0) - 1)
    def _():
        for row in range(ROWS):
            rows = slice(row * share, (row + 1) * share)
            error_new_ref[row] = error_ref[row] - (total[rows, :BLOCK] + total[rows, BLOCK:])


def unsketch(parts, rows, error_mid, tile=1024):
    groups, near, share = len(parts), parts[0].shape[0], parts[0].shape[2]
    quads, _, features = rows.shape
    tile = min(tile, features)
    table_spec = pl.BlockSpec((ROWS, share, BLOCK), lambda i: (0, 0, 0))
    return pl.pallas_call(
        functools.partial(unsketch_kernel, groups, share),
        out_shape=(
            jax.ShapeDtypeStruct((features, quads * BLOCK), jnp.float32),
            jax.ShapeDtypeStruct((ROWS, share, BLOCK), jnp.float32),
        ),
        grid=(features // tile,),
        in_specs=[pl.BlockSpec((near, ROWS, share, BLOCK), lambda i: (0, 0, 0, 0))] * groups
        + [pl.BlockSpec((quads, PAD, tile), lambda i: (0, 0, i)), table_spec],
        out_specs=(pl.BlockSpec((tile, quads * BLOCK), lambda i: (i, 0)), table_spec),
        scratch_shapes=[
            pltpu.VMEM((ROWS * share, 2 * BLOCK), jnp.float32),
            pltpu.VMEM((ROWS, BLOCK, NBB), jnp.bfloat16),
        ],
        compiler_params=params(),
        cost_estimate=SMALL,
        name="unsketch",
    )(*parts, rows, error_mid)


def on_device(hidden_states, gain, key_weight, key_cotangent, bucket, sign_bits, momentum, error):
    fsdp_count = lax.axis_size("fsdp")
    dp_count = lax.axis_size("dp")
    pair = 2 if fsdp_count % 2 == 0 else 1
    turns = fsdp_count // pair
    tokens, width = hidden_states.shape
    quads = key_cotangent.shape[1] // BLOCK
    share = NBB // dp_count
    scale = 1.0 / math.sqrt(tokens * fsdp_count)
    wrap = dp_count & (dp_count - 1) != 0
    near = 1 if wrap or dp_count == 1 else 2
    gain = gain.reshape(1, width)
    decayed = DECAY * momentum.reshape(ROWS, share, BLOCK)
    carried, decayed = lax.optimization_barrier(
        (error.reshape(ROWS, share, BLOCK) + decayed, decayed)
    )

    def across(value):
        return lax.ppermute(value, "fsdp", [(i, i ^ 1) for i in range(fsdp_count)])

    def from_turn(value, step):
        pairs = [
            (((i // pair + step) % turns) * pair + i % pair, i) for i in range(fsdp_count)
        ]
        return lax.ppermute(value, "fsdp", pairs)

    def to_turn(value, step):
        return from_turn(value, turns - step)

    def to_share(value, step):
        return lax.ppermute(value, "dp", [(i, partner(i, step, dp_count)) for i in range(dp_count)])

    def from_share(value, step):
        return lax.ppermute(value, "dp", [(partner(i, step, dp_count), i) for i in range(dp_count)])

    turn_cots = [key_cotangent] + [from_turn(key_cotangent, step) for step in range(1, turns)]
    rows, packed, *inputs = front(
        bucket, sign_bits, hidden_states, gain, quads, wrap, pair, turns
    )
    packed, inputs, turn_cots, cotangent = lax.optimization_barrier(
        (packed, inputs, turn_cots, key_cotangent)
    )
    packed_at = [from_turn(packed, step) for step in range(1, turns)]
    cots, weights = [key_cotangent], [key_weight]
    if pair == 2:
        inputs[1] = across(inputs[1])
        cots.append(across(cotangent))
    first_half, *halves = [(other, half) for other in range(pair) for half in range(HALVES)]
    back = range(turns - 1, 0, -1)
    first_grads = grads(turn_cots, weights, [first_half])
    inputs, first_grads = lax.optimization_barrier((inputs, first_grads))
    first_grads = [first_grads[0]] + [from_turn(first_grads[step], step) for step in back]
    tables = [
        sketch(inputs, cots, packed_at[step - 1], step, scale, dp_count, near)
        for step in range(1, turns)
    ]
    tables, first_grads, weight = lax.optimization_barrier((tables, first_grads, key_weight))
    if pair == 2:
        weights.append(across(weight))
    received = [to_turn(tables[step - 1], step) for step in range(1, turns)]
    table = sketch(inputs, cots, rows, 0, scale, dp_count, near)
    table, turn_cots = lax.optimization_barrier((table, turn_cots))
    table = table.astype(jnp.float32)
    last_grads = grads(turn_cots, weights, halves)
    received, last_grads = lax.optimization_barrier((received, last_grads))
    last_grads = [last_grads[0]] + [from_turn(last_grads[step], step) for step in back]
    grad_parts = first_grads + last_grads
    pieces = [(step, [first_half]) for step in range(turns)]
    pieces += [(step, halves) for step in range(turns)]
    hidden_grad = backward(hidden_states, gain, grad_parts, pieces, turns, pair)

    for other in received:
        table = table + other.astype(jnp.float32)
    if near == 2:
        halves_at = dp_count // near
        arrived = to_share(table[halves_at:].astype(jnp.bfloat16), 1)
        table = table[:halves_at] + arrived.astype(jnp.float32)
    sent = table.astype(jnp.bfloat16)
    total = table[0]
    for step in range(near, dp_count, near):
        total = total + to_share(sent[step // near], step).astype(jnp.float32)
    error_mid = carried + total / dp_count
    error_sent = error_mid.astype(jnp.bfloat16)[None]
    error_sent, total = lax.optimization_barrier((error_sent, total))
    momentum_new = decayed + total / dp_count
    if near == 2:
        error_sent = jnp.concatenate([error_sent, from_share(error_sent, 1)], axis=0)
    parts = [error_sent] + [from_share(error_sent, step) for step in range(near, dp_count, near)]
    parts, hidden_grad = lax.optimization_barrier((parts, hidden_grad))
    update, error_new = unsketch(parts, rows, error_mid)
    return (
        hidden_grad,
        momentum_new.reshape(momentum.shape),
        error_new.reshape(error.shape),
        update,
    )


def solution(mesh):
    in_specs = (
        P(("dp", "fsdp"), None),
        P(),
        P("fsdp", None),
        P(("dp", "fsdp"), None),
        P(None, "fsdp"),
        P(None, "fsdp"),
        P("fsdp", None, "dp"),
        P("fsdp", None, "dp"),
    )
    out_specs = (
        P(("dp", "fsdp"), None),
        P("fsdp", None, "dp"),
        P("fsdp", None, "dp"),
        P("fsdp", None),
    )
    return jax.shard_map(
        on_device, mesh=mesh, in_specs=in_specs, out_specs=out_specs, check_vma=False
    )
```

```python
import functools
import math

import jax
import jax.numpy as jnp
from jax import lax
from jax.experimental import pallas as pl
from jax.experimental.pallas import tpu as pltpu
from jax.sharding import PartitionSpec as P

ROWS = 5
NBB = 256
BLOCK = 128
PAD = 8

EPS = 1e-05
DECAY = 0.9
THRESHOLD = 1.0
MIB = 1024 * 1024
HALVES = 2
SMALL = pl.CostEstimate(flops=1, bytes_accessed=1, transcendentals=0)


def params(limit=48):
    return pltpu.CompilerParams(vmem_limit_bytes=limit * MIB)


def middle_three(first, second, third):
    return jnp.maximum(jnp.minimum(first, second), jnp.minimum(jnp.maximum(first, second), third))


def middle_five(items):
    upper_pair = jnp.minimum(jnp.maximum(items[0], items[1]), jnp.maximum(items[2], items[3]))
    lower_pair = jnp.maximum(jnp.minimum(items[0], items[1]), jnp.minimum(items[2], items[3]))
    return middle_three(items[4], upper_pair, lower_pair)


def picked(code, numbers):
    sign = jnp.where(code < 0, -1.0, 1.0).astype(jnp.bfloat16)
    return jnp.where(jnp.abs(code) == numbers, sign, jnp.zeros((), jnp.bfloat16))


def partner(index, step, count):
    if count & (count - 1) == 0:
        return index ^ step
    return (index + step) % count


def codes(wrap, bucket_ref, sign_ref, rows_ref, packed_ref, stacked, packed):
    share = lax.axis_index("dp") * (NBB // lax.axis_size("dp"))
    quads = rows_ref.shape[0]
    width = quads * BLOCK
    groups = bucket_ref.shape[1] // width
    bucket = bucket_ref[...]
    bucket = lax.rem(bucket + (NBB - share), NBB) if wrap else bucket ^ share
    code = ((bucket + 1) * (2 * sign_ref[...] - 1)).astype(jnp.float32)
    stacked[...] = jnp.zeros_like(stacked)
    for group in range(groups):
        stacked[group * PAD : group * PAD + ROWS, :] = code[:, group * width : (group + 1) * width]
    source = lax.broadcasted_iota(jnp.int32, (width, width), 0)
    target = lax.broadcasted_iota(jnp.int32, (width, width), 1)
    chosen = source == quads * (target % BLOCK) + target // BLOCK
    order = jnp.where(chosen, 1.0, 0.0).astype(jnp.bfloat16)
    moved = jnp.dot(stacked[...].astype(jnp.bfloat16), order, preferred_element_type=jnp.float32)
    for group in range(groups):
        for quad in range(quads):
            part = moved[group * PAD : (group + 1) * PAD, quad * BLOCK : (quad + 1) * BLOCK]
            rows_ref[quad, :, group * BLOCK : (group + 1) * BLOCK] = part.astype(rows_ref.dtype)
            half, place = divmod(group, groups // HALVES)
            first = (quad * HALVES + half) * ROWS
            packed[first : first + ROWS, place * BLOCK : (place + 1) * BLOCK] = part[:ROWS]
    packed_ref[...] = packed[...].astype(packed_ref.dtype)


def front_kernel(wrap, pair, turns, bucket_ref, sign_ref, hidden_ref, gain_ref, *refs):
    rows_ref, packed_ref, out_refs = refs[0], refs[1], refs[2 : 2 + pair]

    @pl.when(pl.program_id(0) == 0)
    def _():
        codes(wrap, bucket_ref, sign_ref, rows_ref, packed_ref, *refs[2 + pair :])

    fsdp_at = lax.axis_index("fsdp")
    core, place = lax.rem(fsdp_at, pair), fsdp_at // pair
    features = out_refs[0].shape[2]
    tile, width = hidden_ref.shape
    squares = jnp.zeros((tile, BLOCK), jnp.float32)
    for part in range(0, width, BLOCK):
        values = hidden_ref[:, part : part + BLOCK].astype(jnp.float32)
        squares += values * values
    inverse_rms = lax.rsqrt(jnp.sum(squares, axis=1, keepdims=True) / width + EPS)
    for other in range(pair):
        for step in range(turns):
            slab = lax.rem(place + step, turns) * pair + (core ^ other)
            for part in range(0, features, 2 * BLOCK):
                span = pl.ds(pl.multiple_of(slab * features + part, BLOCK), 2 * BLOCK)
                normed = hidden_ref[:, span].astype(jnp.float32) * inverse_rms
                out_refs[other][step, :, part : part + 2 * BLOCK] = (
                    normed * gain_ref[:, span]
                ).astype(jnp.bfloat16)


def front(bucket, sign_bits, hidden, gain, quads, wrap, pair, turns, tile=64):
    tokens, width = hidden.shape
    features = width // (pair * turns)
    tile = min(tokens, tile)
    out = jax.ShapeDtypeStruct((turns, tokens, features), jnp.bfloat16)
    packed = (quads * HALVES * ROWS, features // HALVES)
    return pl.pallas_call(
        functools.partial(front_kernel, wrap, pair, turns),
        out_shape=(
            jax.ShapeDtypeStruct((quads, PAD, features), jnp.bfloat16),
            jax.ShapeDtypeStruct(packed, jnp.bfloat16),
        )
        + (out,) * pair,
        grid=(tokens // tile,),
        in_specs=[
            pl.BlockSpec(bucket.shape, lambda i: (0, 0)),
            pl.BlockSpec(bucket.shape, lambda i: (0, 0)),
            pl.BlockSpec((tile, width), lambda i: (i, 0)),
            pl.BlockSpec((1, width), lambda i: (0, 0)),
        ],
        out_specs=(
            pl.BlockSpec((quads, PAD, features), lambda i: (0, 0, 0)),
            pl.BlockSpec(packed, lambda i: (0, 0)),
        )
        + (pl.BlockSpec((turns, tile, features), lambda i: (0, i, 0)),) * pair,
        scratch_shapes=[
            pltpu.VMEM((features // BLOCK * PAD, quads * BLOCK), jnp.float32),
            pltpu.VMEM(packed, jnp.float32),
        ],
        compiler_params=params(60),
        cost_estimate=SMALL,
        name="codes_and_normed",
    )(bucket, sign_bits, hidden, gain)


def sketch_kernel(scale, count, near, pair, quads, *refs):
    inputs_refs, cot_refs, rows_ref = refs[:pair], refs[pair : 2 * pair], refs[2 * pair]
    table_ref = refs[2 * pair + 1]
    contract = (((0,), (0,)), ((), ()))
    inputs = jnp.concatenate([ref[0] for ref in inputs_refs], axis=0)
    cots = jnp.concatenate([ref[...] for ref in cot_refs], axis=0)
    grad = lax.dot_general(inputs, cots, contract, preferred_element_type=jnp.float32)
    upper = grad.astype(jnp.bfloat16)
    lower = (grad - upper.astype(jnp.float32)).astype(jnp.bfloat16)
    both = jnp.concatenate(
        [
            jnp.concatenate(
                [part[:, quad * BLOCK : (quad + 1) * BLOCK] for part in (upper, lower)], axis=1
            )
            for quad in range(quads)
        ],
        axis=0,
    )
    features = inputs.shape[1]
    pieces = 1 if len(rows_ref.shape) == 3 else HALVES
    numbers = lax.broadcasted_iota(jnp.int32, (NBB, features // pieces), 0)
    numbers = numbers.astype(jnp.bfloat16) + 1
    share = NBB // count
    for row in range(ROWS):
        picks = []
        for quad in range(quads):
            for piece in range(pieces):
                if pieces == 1:
                    code = rows_ref[quad, row : row + 1, :]
                else:
                    at = (quad * HALVES + piece) * ROWS + row
                    code = rows_ref[at : at + 1, :]
                picks.append(picked(code, numbers))
        pick = jnp.concatenate(picks, axis=1)
        sums = jnp.dot(pick, both, preferred_element_type=jnp.float32)
        table = (sums[:, :BLOCK] + sums[:, BLOCK:]) * scale
        for part in range(count):
            table_ref[part % near * (count // near) + part // near, row] = table[part * share : (part + 1) * share, :].astype(
                table_ref.dtype
            )


def sketch(inputs, cots, rows, which, scale, count, near):
    tokens, features = inputs[0].shape[1:]
    quads = cots[0].shape[1] // BLOCK
    pair = len(inputs)
    table = (count, ROWS, NBB // count, BLOCK)
    return pl.pallas_call(
        functools.partial(sketch_kernel, scale, count, near, pair, quads),
        out_shape=jax.ShapeDtypeStruct(table, jnp.bfloat16),
        grid=(1,),
        in_specs=[pl.BlockSpec((1, tokens, features), lambda i: (which, 0, 0))] * pair
        + [pl.BlockSpec(cots[0].shape, lambda i: (0, 0))] * pair
        + [pl.BlockSpec(rows.shape, lambda i: (0,) * rows.ndim)],
        out_specs=pl.BlockSpec(table, lambda i: (0, 0, 0, 0)),
        compiler_params=params(),
        cost_estimate=pl.CostEstimate(
            flops=4 * ROWS * NBB * quads * features * BLOCK,
            bytes_accessed=4 * pair * tokens * features,
            transcendentals=0,
        ),
        name="sketch",
    )(*inputs, *cots, rows)


def grads_kernel(turns, *refs):
    cot_refs, weight_refs, out_refs = refs[:turns], refs[turns:-turns], refs[-turns:]
    cots = jnp.concatenate([ref[...] for ref in cot_refs], axis=0)
    tokens = cot_refs[0].shape[0]
    for index, weight_ref in enumerate(weight_refs):
        grad = lax.dot_general(
            cots, weight_ref[...], (((1,), (1,)), ((), ())), preferred_element_type=jnp.float32
        ).astype(jnp.bfloat16)
        for step in range(turns):
            out_refs[step][index] = grad[step * tokens : (step + 1) * tokens]


def grads(cots, weights, pieces):
    turns = len(cots)
    tokens, width = cots[0].shape
    size = weights[0].shape[0] // HALVES
    out = (len(pieces), tokens, size)
    return pl.pallas_call(
        functools.partial(grads_kernel, turns),
        out_shape=(jax.ShapeDtypeStruct(out, jnp.bfloat16),) * turns,
        grid=(1,),
        in_specs=[pl.BlockSpec((tokens, width), lambda i: (0, 0))] * turns
        + [
            pl.BlockSpec((size, width), functools.partial(lambda half, i: (half, 0), half))
            for _, half in pieces
        ],
        out_specs=(pl.BlockSpec(out, lambda i: (0, 0, 0)),) * turns,
        compiler_params=params(),
        cost_estimate=SMALL,
        name="input_grad",
    )(*cots, *[weights[other] for other, _ in pieces])


def backward_kernel(turns, pair, pieces, hidden_ref, gain_ref, *refs):
    grad_refs, out_ref = refs[:-1], refs[-1]
    fsdp_at = lax.axis_index("fsdp")
    core, place = lax.rem(fsdp_at, pair), fsdp_at // pair
    width = hidden_ref.shape[1]
    features = width // (turns * pair)
    size = features // HALVES
    spans = []
    squares = jnp.zeros((hidden_ref.shape[0], BLOCK), jnp.float32)
    products = squares
    for (step, halves), grad_ref in zip(pieces, grad_refs):
        for index, (other, half) in enumerate(halves):
            slab = lax.rem(place + step, turns) * pair + (core ^ other)
            start = slab * features + half * size
            for part in range(0, size, BLOCK):
                span = pl.ds(pl.multiple_of(start + part, BLOCK), BLOCK)
                values = hidden_ref[:, span].astype(jnp.float32)
                grad = grad_ref[index, :, part : part + BLOCK].astype(jnp.float32)
                squares += values * values
                products += grad * gain_ref[:, span] * values
            spans.append((grad_ref, index, pl.ds(pl.multiple_of(start, BLOCK), size)))
    inverse_rms = lax.rsqrt(jnp.sum(squares, axis=1, keepdims=True) / width + EPS)
    mean_term = inverse_rms * jnp.sum(products, axis=1, keepdims=True) / width
    shrink = inverse_rms * (inverse_rms * mean_term)
    for grad_ref, index, span in spans:
        scaled = grad_ref[index].astype(jnp.float32) * gain_ref[:, span]
        values = hidden_ref[:, span].astype(jnp.float32)
        out_ref[:, span] = (inverse_rms * scaled - shrink * values).astype(jnp.bfloat16)


def backward(hidden, gain, grad_parts, pieces, turns, pair, tile=32):
    tokens, width = hidden.shape
    tile = min(tokens, tile)
    return pl.pallas_call(
        functools.partial(backward_kernel, turns, pair, pieces),
        out_shape=jax.ShapeDtypeStruct((tokens, width), jnp.bfloat16),
        grid=(tokens // tile,),
        in_specs=[
            pl.BlockSpec((tile, width), lambda i: (i, 0)),
            pl.BlockSpec((1, width), lambda i: (0, 0)),
        ]
        + [
            pl.BlockSpec((part.shape[0], tile, part.shape[2]), lambda i: (0, i, 0))
            for part in grad_parts
        ],
        out_specs=pl.BlockSpec((tile, width), lambda i: (i, 0)),
        compiler_params=params(),
        cost_estimate=SMALL,
        name="hidden_grad",
    )(hidden, gain, *grad_parts)


def unsketch_kernel(groups, share, *refs):
    part_refs, rows_ref, error_ref = refs[:groups], *refs[groups : groups + 2]
    update_ref, error_new_ref, total, tables = refs[groups + 2 :]
    step = pl.program_id(0)
    quads, tile = rows_ref.shape[0], rows_ref.shape[2]
    numbers = lax.broadcasted_iota(jnp.int32, (NBB, tile), 0).astype(jnp.bfloat16) + 1

    @pl.when(step == 0)
    def _():
        total[...] = jnp.zeros_like(total)
        for row in range(ROWS):
            table = jnp.concatenate(
                [ref[near, row] for ref in part_refs for near in range(ref.shape[0])], axis=0
            )
            tables[row] = table.astype(jnp.float32).T.astype(jnp.bfloat16)

    for quad in range(quads):
        reads, own = [], []
        for row in range(ROWS):
            pick = picked(rows_ref[quad, row : row + 1, :], numbers)
            own.append(pick[:share])
            reads.append(jnp.dot(tables[row], pick, preferred_element_type=jnp.float32))
        estimate = middle_five(reads)
        update = (estimate - jnp.clip(estimate, -THRESHOLD, THRESHOLD)).T
        update_ref[:, quad * BLOCK : (quad + 1) * BLOCK] = update
        upper = update.astype(jnp.bfloat16)
        lower = (update - upper.astype(jnp.float32)).astype(jnp.bfloat16)
        both = jnp.concatenate([upper, lower], axis=1)
        total[...] += jnp.dot(
            jnp.concatenate(own, axis=0), both, preferred_element_type=jnp.float32
        )

    @pl.when(step == pl.num_programs(0) - 1)
    def _():
        for row in range(ROWS):
            rows = slice(row * share, (row + 1) * share)
            error_new_ref[row] = error_ref[row] - (total[rows, :BLOCK] + total[rows, BLOCK:])


def unsketch(parts, rows, error_mid, tile=1024):
    groups, near, share = len(parts), parts[0].shape[0], parts[0].shape[2]
    quads, _, features = rows.shape
    tile = min(tile, features)
    table_spec = pl.BlockSpec((ROWS, share, BLOCK), lambda i: (0, 0, 0))
    return pl.pallas_call(
        functools.partial(unsketch_kernel, groups, share),
        out_shape=(
            jax.ShapeDtypeStruct((features, quads * BLOCK), jnp.float32),
            jax.ShapeDtypeStruct((ROWS, share, BLOCK), jnp.float32),
        ),
        grid=(features // tile,),
        in_specs=[pl.BlockSpec((near, ROWS, share, BLOCK), lambda i: (0, 0, 0, 0))] * groups
        + [pl.BlockSpec((quads, PAD, tile), lambda i: (0, 0, i)), table_spec],
        out_specs=(pl.BlockSpec((tile, quads * BLOCK), lambda i: (i, 0)), table_spec),
        scratch_shapes=[
            pltpu.VMEM((ROWS * share, 2 * BLOCK), jnp.float32),
            pltpu.VMEM((ROWS, BLOCK, NBB), jnp.bfloat16),
        ],
        compiler_params=params(),
        cost_estimate=SMALL,
        name="unsketch",
    )(*parts, rows, error_mid)


def on_device(hidden_states, gain, key_weight, key_cotangent, bucket, sign_bits, momentum, error):
    fsdp_count = lax.axis_size("fsdp")
    dp_count = lax.axis_size("dp")
    pair = 2 if fsdp_count % 2 == 0 else 1
    turns = fsdp_count // pair
    tokens, width = hidden_states.shape
    quads = key_cotangent.shape[1] // BLOCK
    share = NBB // dp_count
    scale = 1.0 / math.sqrt(tokens * fsdp_count)
    wrap = dp_count & (dp_count - 1) != 0
    near = 1 if wrap or dp_count == 1 else 2
    gain = gain.reshape(1, width)
    decayed = DECAY * momentum.reshape(ROWS, share, BLOCK)
    carried, decayed = lax.optimization_barrier(
        (error.reshape(ROWS, share, BLOCK) + decayed, decayed)
    )

    def across(value):
        return lax.ppermute(value, "fsdp", [(i, i ^ 1) for i in range(fsdp_count)])

    def from_turn(value, step):
        pairs = [
            (((i // pair + step) % turns) * pair + i % pair, i) for i in range(fsdp_count)
        ]
        return lax.ppermute(value, "fsdp", pairs)

    def to_turn(value, step):
        return from_turn(value, turns - step)

    def to_share(value, step):
        return lax.ppermute(value, "dp", [(i, partner(i, step, dp_count)) for i in range(dp_count)])

    def from_share(value, step):
        return lax.ppermute(value, "dp", [(partner(i, step, dp_count), i) for i in range(dp_count)])

    turn_cots = [key_cotangent] + [from_turn(key_cotangent, step) for step in range(1, turns)]
    rows, packed, *inputs = front(
        bucket, sign_bits, hidden_states, gain, quads, wrap, pair, turns
    )
    packed, inputs, turn_cots, cotangent = lax.optimization_barrier(
        (packed, inputs, turn_cots, key_cotangent)
    )
    packed_at = [from_turn(packed, step) for step in range(1, turns)]
    cots, weights = [key_cotangent], [key_weight]
    if pair == 2:
        inputs[1] = across(inputs[1])
        cots.append(across(cotangent))
    first_half, *halves = [(other, half) for other in range(pair) for half in range(HALVES)]
    back = range(turns - 1, 0, -1)
    first_grads = grads(turn_cots, weights, [first_half])
    inputs, first_grads = lax.optimization_barrier((inputs, first_grads))
    first_grads = [first_grads[0]] + [from_turn(first_grads[step], step) for step in back]
    tables = [
        sketch(inputs, cots, packed_at[step - 1], step, scale, dp_count, near)
        for step in range(1, turns)
    ]
    tables, first_grads, weight = lax.optimization_barrier((tables, first_grads, key_weight))
    if pair == 2:
        weights.append(across(weight))
    received = [to_turn(tables[step - 1], step) for step in range(1, turns)]
    table = sketch(inputs, cots, rows, 0, scale, dp_count, near)
    table, turn_cots = lax.optimization_barrier((table, turn_cots))
    table = table.astype(jnp.float32)
    last_grads = grads(turn_cots, weights, halves)
    received, last_grads = lax.optimization_barrier((received, last_grads))
    last_grads = [last_grads[0]] + [from_turn(last_grads[step], step) for step in back]
    grad_parts = first_grads + last_grads
    pieces = [(step, [first_half]) for step in range(turns)]
    pieces += [(step, halves) for step in range(turns)]
    hidden_grad = backward(hidden_states, gain, grad_parts, pieces, turns, pair)

    for other in received:
        table = table + other.astype(jnp.float32)
    if near == 2:
        halves_at = dp_count // near
        arrived = to_share(table[halves_at:].astype(jnp.bfloat16), 1)
        table = table[:halves_at] + arrived.astype(jnp.float32)
    sent = table.astype(jnp.bfloat16)
    total = table[0]
    for step in range(dp_count - near, 0, -near):
        total = total + to_share(sent[step // near], step).astype(jnp.float32)
    error_mid = carried + total / dp_count
    error_sent = error_mid.astype(jnp.bfloat16)[None]
    error_sent, total = lax.optimization_barrier((error_sent, total))
    momentum_new = decayed + total / dp_count
    if near == 2:
        error_sent = jnp.concatenate([error_sent, from_share(error_sent, 1)], axis=0)
    parts = [error_sent] + [from_share(error_sent, step) for step in range(near, dp_count, near)]
    parts, hidden_grad = lax.optimization_barrier((parts, hidden_grad))
    update, error_new = unsketch(parts, rows, error_mid)
    return (
        hidden_grad,
        momentum_new.reshape(momentum.shape),
        error_new.reshape(error.shape),
        update,
    )


def solution(mesh):
    in_specs = (
        P(("dp", "fsdp"), None),
        P(),
        P("fsdp", None),
        P(("dp", "fsdp"), None),
        P(None, "fsdp"),
        P(None, "fsdp"),
        P("fsdp", None, "dp"),
        P("fsdp", None, "dp"),
    )
    out_specs = (
        P(("dp", "fsdp"), None),
        P("fsdp", None, "dp"),
        P("fsdp", None, "dp"),
        P("fsdp", None),
    )
    return jax.shard_map(
        on_device, mesh=mesh, in_specs=in_specs, out_specs=out_specs, check_vma=False
    )
```

```python
import functools
import math

import jax
import jax.numpy as jnp
from jax import lax
from jax.experimental import pallas as pl
from jax.experimental.pallas import tpu as pltpu
from jax.sharding import PartitionSpec as P

ROWS = 5
NBB = 256
BLOCK = 128
PAD = 8

EPS = 1e-05
DECAY = 0.9
THRESHOLD = 1.0
MIB = 1024 * 1024
HALVES = 2
SMALL = pl.CostEstimate(flops=1, bytes_accessed=1, transcendentals=0)


def params(limit=48):
    return pltpu.CompilerParams(vmem_limit_bytes=limit * MIB)


def middle_three(first, second, third):
    return jnp.maximum(jnp.minimum(first, second), jnp.minimum(jnp.maximum(first, second), third))


def middle_five(items):
    upper_pair = jnp.minimum(jnp.maximum(items[0], items[1]), jnp.maximum(items[2], items[3]))
    lower_pair = jnp.maximum(jnp.minimum(items[0], items[1]), jnp.minimum(items[2], items[3]))
    return middle_three(items[4], upper_pair, lower_pair)


def picked(code, numbers):
    sign = jnp.where(code < 0, -1.0, 1.0).astype(jnp.bfloat16)
    return jnp.where(jnp.abs(code) == numbers, sign, jnp.zeros((), jnp.bfloat16))


def partner(index, step, count):
    if count & (count - 1) == 0:
        return index ^ step
    return (index + step) % count


def codes(wrap, bucket_ref, sign_ref, rows_ref, packed_ref, stacked, packed):
    share = lax.axis_index("dp") * (NBB // lax.axis_size("dp"))
    quads = rows_ref.shape[0]
    width = quads * BLOCK
    groups = bucket_ref.shape[1] // width
    bucket = bucket_ref[...]
    bucket = lax.rem(bucket + (NBB - share), NBB) if wrap else bucket ^ share
    code = ((bucket + 1) * (2 * sign_ref[...] - 1)).astype(jnp.float32)
    stacked[...] = jnp.zeros_like(stacked)
    for group in range(groups):
        stacked[group * PAD : group * PAD + ROWS, :] = code[:, group * width : (group + 1) * width]
    source = lax.broadcasted_iota(jnp.int32, (width, width), 0)
    target = lax.broadcasted_iota(jnp.int32, (width, width), 1)
    chosen = source == quads * (target % BLOCK) + target // BLOCK
    order = jnp.where(chosen, 1.0, 0.0).astype(jnp.bfloat16)
    moved = jnp.dot(stacked[...].astype(jnp.bfloat16), order, preferred_element_type=jnp.float32)
    for group in range(groups):
        for quad in range(quads):
            part = moved[group * PAD : (group + 1) * PAD, quad * BLOCK : (quad + 1) * BLOCK]
            rows_ref[quad, :, group * BLOCK : (group + 1) * BLOCK] = part.astype(rows_ref.dtype)
            half, place = divmod(group, groups // HALVES)
            first = (quad * HALVES + half) * ROWS
            packed[first : first + ROWS, place * BLOCK : (place + 1) * BLOCK] = part[:ROWS]
    packed_ref[...] = packed[...].astype(packed_ref.dtype)


def front_kernel(wrap, pair, turns, bucket_ref, sign_ref, hidden_ref, gain_ref, *refs):
    rows_ref, packed_ref, out_refs = refs[0], refs[1], refs[2 : 2 + pair]

    @pl.when(pl.program_id(0) == 0)
    def _():
        codes(wrap, bucket_ref, sign_ref, rows_ref, packed_ref, *refs[2 + pair :])

    fsdp_at = lax.axis_index("fsdp")
    core, place = lax.rem(fsdp_at, pair), fsdp_at // pair
    features = out_refs[0].shape[2]
    tile, width = hidden_ref.shape
    squares = jnp.zeros((tile, BLOCK), jnp.float32)
    for part in range(0, width, BLOCK):
        values = hidden_ref[:, part : part + BLOCK].astype(jnp.float32)
        squares += values * values
    inverse_rms = lax.rsqrt(jnp.sum(squares, axis=1, keepdims=True) / width + EPS)
    for other in range(pair):
        for step in range(turns):
            slab = lax.rem(place + step, turns) * pair + (core ^ other)
            for part in range(0, features, 2 * BLOCK):
                span = pl.ds(pl.multiple_of(slab * features + part, BLOCK), 2 * BLOCK)
                normed = hidden_ref[:, span].astype(jnp.float32) * inverse_rms
                out_refs[other][step, :, part : part + 2 * BLOCK] = (
                    normed * gain_ref[:, span]
                ).astype(jnp.bfloat16)


def front(bucket, sign_bits, hidden, gain, quads, wrap, pair, turns, tile=64):
    tokens, width = hidden.shape
    features = width // (pair * turns)
    tile = min(tokens, tile)
    out = jax.ShapeDtypeStruct((turns, tokens, features), jnp.bfloat16)
    packed = (quads * HALVES * ROWS, features // HALVES)
    return pl.pallas_call(
        functools.partial(front_kernel, wrap, pair, turns),
        out_shape=(
            jax.ShapeDtypeStruct((quads, PAD, features), jnp.bfloat16),
            jax.ShapeDtypeStruct(packed, jnp.bfloat16),
        )
        + (out,) * pair,
        grid=(tokens // tile,),
        in_specs=[
            pl.BlockSpec(bucket.shape, lambda i: (0, 0)),
            pl.BlockSpec(bucket.shape, lambda i: (0, 0)),
            pl.BlockSpec((tile, width), lambda i: (i, 0)),
            pl.BlockSpec((1, width), lambda i: (0, 0)),
        ],
        out_specs=(
            pl.BlockSpec((quads, PAD, features), lambda i: (0, 0, 0)),
            pl.BlockSpec(packed, lambda i: (0, 0)),
        )
        + (pl.BlockSpec((turns, tile, features), lambda i: (0, i, 0)),) * pair,
        scratch_shapes=[
            pltpu.VMEM((features // BLOCK * PAD, quads * BLOCK), jnp.float32),
            pltpu.VMEM(packed, jnp.float32),
        ],
        compiler_params=params(60),
        cost_estimate=SMALL,
        name="codes_and_normed",
    )(bucket, sign_bits, hidden, gain)


def sketch_kernel(scale, count, near, pair, quads, *refs):
    inputs_refs, cot_refs, rows_ref = refs[:pair], refs[pair : 2 * pair], refs[2 * pair]
    table_ref = refs[2 * pair + 1]
    contract = (((0,), (0,)), ((), ()))
    inputs = jnp.concatenate([ref[0] for ref in inputs_refs], axis=0)
    cots = jnp.concatenate([ref[...] for ref in cot_refs], axis=0)
    grad = lax.dot_general(inputs, cots, contract, preferred_element_type=jnp.float32)
    upper = grad.astype(jnp.bfloat16)
    lower = (grad - upper.astype(jnp.float32)).astype(jnp.bfloat16)
    both = jnp.concatenate(
        [
            jnp.concatenate(
                [part[:, quad * BLOCK : (quad + 1) * BLOCK] for part in (upper, lower)], axis=1
            )
            for quad in range(quads)
        ],
        axis=0,
    )
    features = inputs.shape[1]
    pieces = 1 if len(rows_ref.shape) == 3 else HALVES
    numbers = lax.broadcasted_iota(jnp.int32, (NBB, features // pieces), 0)
    numbers = numbers.astype(jnp.bfloat16) + 1
    share = NBB // count
    for row in range(ROWS):
        picks = []
        for quad in range(quads):
            for piece in range(pieces):
                if pieces == 1:
                    code = rows_ref[quad, row : row + 1, :]
                else:
                    at = (quad * HALVES + piece) * ROWS + row
                    code = rows_ref[at : at + 1, :]
                picks.append(picked(code, numbers))
        pick = jnp.concatenate(picks, axis=1)
        sums = jnp.dot(pick, both, preferred_element_type=jnp.float32)
        table = (sums[:, :BLOCK] + sums[:, BLOCK:]) * scale
        for part in range(count):
            table_ref[part % near * (count // near) + part // near, row] = table[part * share : (part + 1) * share, :].astype(
                table_ref.dtype
            )


def sketch(inputs, cots, rows, which, scale, count, near):
    tokens, features = inputs[0].shape[1:]
    quads = cots[0].shape[1] // BLOCK
    pair = len(inputs)
    table = (count, ROWS, NBB // count, BLOCK)
    return pl.pallas_call(
        functools.partial(sketch_kernel, scale, count, near, pair, quads),
        out_shape=jax.ShapeDtypeStruct(table, jnp.bfloat16),
        grid=(1,),
        in_specs=[pl.BlockSpec((1, tokens, features), lambda i: (which, 0, 0))] * pair
        + [pl.BlockSpec(cots[0].shape, lambda i: (0, 0))] * pair
        + [pl.BlockSpec(rows.shape, lambda i: (0,) * rows.ndim)],
        out_specs=pl.BlockSpec(table, lambda i: (0, 0, 0, 0)),
        compiler_params=params(),
        cost_estimate=pl.CostEstimate(
            flops=4 * ROWS * NBB * quads * features * BLOCK,
            bytes_accessed=4 * pair * tokens * features,
            transcendentals=0,
        ),
        name="sketch",
    )(*inputs, *cots, rows)


def grads_kernel(turns, *refs):
    cot_refs, weight_refs, out_refs = refs[:turns], refs[turns:-turns], refs[-turns:]
    cots = jnp.concatenate([ref[...] for ref in cot_refs], axis=0)
    tokens = cot_refs[0].shape[0]
    for index, weight_ref in enumerate(weight_refs):
        grad = lax.dot_general(
            cots, weight_ref[...], (((1,), (1,)), ((), ())), preferred_element_type=jnp.float32
        ).astype(jnp.bfloat16)
        for step in range(turns):
            out_refs[step][index] = grad[step * tokens : (step + 1) * tokens]


def grads(cots, weights, pieces):
    turns = len(cots)
    tokens, width = cots[0].shape
    size = weights[0].shape[0] // HALVES
    out = (len(pieces), tokens, size)
    return pl.pallas_call(
        functools.partial(grads_kernel, turns),
        out_shape=(jax.ShapeDtypeStruct(out, jnp.bfloat16),) * turns,
        grid=(1,),
        in_specs=[pl.BlockSpec((tokens, width), lambda i: (0, 0))] * turns
        + [
            pl.BlockSpec((size, width), functools.partial(lambda half, i: (half, 0), half))
            for _, half in pieces
        ],
        out_specs=(pl.BlockSpec(out, lambda i: (0, 0, 0)),) * turns,
        compiler_params=params(),
        cost_estimate=SMALL,
        name="input_grad",
    )(*cots, *[weights[other] for other, _ in pieces])


def backward_kernel(turns, pair, pieces, hidden_ref, gain_ref, *refs):
    grad_refs, out_ref = refs[:-1], refs[-1]
    fsdp_at = lax.axis_index("fsdp")
    core, place = lax.rem(fsdp_at, pair), fsdp_at // pair
    width = hidden_ref.shape[1]
    features = width // (turns * pair)
    size = features // HALVES
    spans = []
    squares = jnp.zeros((hidden_ref.shape[0], BLOCK), jnp.float32)
    products = squares
    for (step, halves), grad_ref in zip(pieces, grad_refs):
        for index, (other, half) in enumerate(halves):
            slab = lax.rem(place + step, turns) * pair + (core ^ other)
            start = slab * features + half * size
            for part in range(0, size, BLOCK):
                span = pl.ds(pl.multiple_of(start + part, BLOCK), BLOCK)
                values = hidden_ref[:, span].astype(jnp.float32)
                grad = grad_ref[index, :, part : part + BLOCK].astype(jnp.float32)
                squares += values * values
                products += grad * gain_ref[:, span] * values
            spans.append((grad_ref, index, pl.ds(pl.multiple_of(start, BLOCK), size)))
    inverse_rms = lax.rsqrt(jnp.sum(squares, axis=1, keepdims=True) / width + EPS)
    mean_term = inverse_rms * jnp.sum(products, axis=1, keepdims=True) / width
    shrink = inverse_rms * (inverse_rms * mean_term)
    for grad_ref, index, span in spans:
        scaled = grad_ref[index].astype(jnp.float32) * gain_ref[:, span]
        values = hidden_ref[:, span].astype(jnp.float32)
        out_ref[:, span] = (inverse_rms * scaled - shrink * values).astype(jnp.bfloat16)


def backward(hidden, gain, grad_parts, pieces, turns, pair, tile=32):
    tokens, width = hidden.shape
    tile = min(tokens, tile)
    return pl.pallas_call(
        functools.partial(backward_kernel, turns, pair, pieces),
        out_shape=jax.ShapeDtypeStruct((tokens, width), jnp.bfloat16),
        grid=(tokens // tile,),
        in_specs=[
            pl.BlockSpec((tile, width), lambda i: (i, 0)),
            pl.BlockSpec((1, width), lambda i: (0, 0)),
        ]
        + [
            pl.BlockSpec((part.shape[0], tile, part.shape[2]), lambda i: (0, i, 0))
            for part in grad_parts
        ],
        out_specs=pl.BlockSpec((tile, width), lambda i: (i, 0)),
        compiler_params=params(),
        cost_estimate=SMALL,
        name="hidden_grad",
    )(hidden, gain, *grad_parts)


def unsketch_kernel(groups, share, *refs):
    part_refs, rows_ref, error_ref = refs[:groups], *refs[groups : groups + 2]
    update_ref, error_new_ref, total, tables = refs[groups + 2 :]
    step = pl.program_id(0)
    quads, tile = rows_ref.shape[0], rows_ref.shape[2]
    numbers = lax.broadcasted_iota(jnp.int32, (NBB, tile), 0).astype(jnp.bfloat16) + 1

    @pl.when(step == 0)
    def _():
        total[...] = jnp.zeros_like(total)
        for row in range(ROWS):
            table = jnp.concatenate(
                [ref[near, row] for ref in part_refs for near in range(ref.shape[0])], axis=0
            )
            tables[row] = table.astype(jnp.float32).T.astype(jnp.bfloat16)

    for quad in range(quads):
        reads, own = [], []
        for row in range(ROWS):
            pick = picked(rows_ref[quad, row : row + 1, :], numbers)
            own.append(pick[:share])
            reads.append(jnp.dot(tables[row], pick, preferred_element_type=jnp.float32))
        estimate = middle_five(reads)
        update = (estimate - jnp.clip(estimate, -THRESHOLD, THRESHOLD)).T
        update_ref[:, quad * BLOCK : (quad + 1) * BLOCK] = update
        upper = update.astype(jnp.bfloat16)
        lower = (update - upper.astype(jnp.float32)).astype(jnp.bfloat16)
        both = jnp.concatenate([upper, lower], axis=1)
        total[...] += jnp.dot(
            jnp.concatenate(own, axis=0), both, preferred_element_type=jnp.float32
        )

    @pl.when(step == pl.num_programs(0) - 1)
    def _():
        for row in range(ROWS):
            rows = slice(row * share, (row + 1) * share)
            error_new_ref[row] = error_ref[row] - (total[rows, :BLOCK] + total[rows, BLOCK:])


def unsketch(parts, rows, error_mid, tile=1024):
    groups, near, share = len(parts), parts[0].shape[0], parts[0].shape[2]
    quads, _, features = rows.shape
    tile = min(tile, features)
    table_spec = pl.BlockSpec((ROWS, share, BLOCK), lambda i: (0, 0, 0))
    return pl.pallas_call(
        functools.partial(unsketch_kernel, groups, share),
        out_shape=(
            jax.ShapeDtypeStruct((features, quads * BLOCK), jnp.float32),
            jax.ShapeDtypeStruct((ROWS, share, BLOCK), jnp.float32),
        ),
        grid=(features // tile,),
        in_specs=[pl.BlockSpec((near, ROWS, share, BLOCK), lambda i: (0, 0, 0, 0))] * groups
        + [pl.BlockSpec((quads, PAD, tile), lambda i: (0, 0, i)), table_spec],
        out_specs=(pl.BlockSpec((tile, quads * BLOCK), lambda i: (i, 0)), table_spec),
        scratch_shapes=[
            pltpu.VMEM((ROWS * share, 2 * BLOCK), jnp.float32),
            pltpu.VMEM((ROWS, BLOCK, NBB), jnp.bfloat16),
        ],
        compiler_params=params(),
        cost_estimate=SMALL,
        name="unsketch",
    )(*parts, rows, error_mid)


def on_device(hidden_states, gain, key_weight, key_cotangent, bucket, sign_bits, momentum, error):
    fsdp_count = lax.axis_size("fsdp")
    dp_count = lax.axis_size("dp")
    pair = 2 if fsdp_count % 2 == 0 else 1
    turns = fsdp_count // pair
    tokens, width = hidden_states.shape
    quads = key_cotangent.shape[1] // BLOCK
    share = NBB // dp_count
    scale = 1.0 / math.sqrt(tokens * fsdp_count)
    wrap = dp_count & (dp_count - 1) != 0
    near = 1 if wrap or dp_count == 1 else 2
    gain = gain.reshape(1, width)
    decayed = DECAY * momentum.reshape(ROWS, share, BLOCK)
    carried, decayed = lax.optimization_barrier(
        (error.reshape(ROWS, share, BLOCK) + decayed, decayed)
    )

    def across(value):
        return lax.ppermute(value, "fsdp", [(i, i ^ 1) for i in range(fsdp_count)])

    def from_turn(value, step):
        pairs = [
            (((i // pair + step) % turns) * pair + i % pair, i) for i in range(fsdp_count)
        ]
        return lax.ppermute(value, "fsdp", pairs)

    def to_turn(value, step):
        return from_turn(value, turns - step)

    def to_share(value, step):
        return lax.ppermute(value, "dp", [(i, partner(i, step, dp_count)) for i in range(dp_count)])

    def from_share(value, step):
        return lax.ppermute(value, "dp", [(partner(i, step, dp_count), i) for i in range(dp_count)])

    turn_cots = [key_cotangent] + [from_turn(key_cotangent, step) for step in range(1, turns)]
    rows, packed, *inputs = front(
        bucket, sign_bits, hidden_states, gain, quads, wrap, pair, turns
    )
    packed, inputs, turn_cots, cotangent = lax.optimization_barrier(
        (packed, inputs, turn_cots, key_cotangent)
    )
    packed_at = [from_turn(packed, step) for step in range(1, turns)]
    cots, weights = [key_cotangent], [key_weight]
    if pair == 2:
        inputs[1] = across(inputs[1])
        inputs, cotangent = lax.optimization_barrier((inputs, cotangent))
        cots.append(across(cotangent))
    first_half, *halves = [(other, half) for other in range(pair) for half in range(HALVES)]
    back = range(turns - 1, 0, -1)
    first_grads = grads(turn_cots, weights, [first_half])
    inputs, first_grads = lax.optimization_barrier((inputs, first_grads))
    first_grads = [first_grads[0]] + [from_turn(first_grads[step], step) for step in back]
    tables = [
        sketch(inputs, cots, packed_at[step - 1], step, scale, dp_count, near)
        for step in range(1, turns)
    ]
    tables, first_grads, weight = lax.optimization_barrier((tables, first_grads, key_weight))
    if pair == 2:
        weights.append(across(weight))
    received = [to_turn(tables[step - 1], step) for step in range(1, turns)]
    table = sketch(inputs, cots, rows, 0, scale, dp_count, near)
    table, turn_cots = lax.optimization_barrier((table, turn_cots))
    table = table.astype(jnp.float32)
    last_grads = grads(turn_cots, weights, halves)
    received, last_grads = lax.optimization_barrier((received, last_grads))
    last_grads = [last_grads[0]] + [from_turn(last_grads[step], step) for step in back]
    grad_parts = first_grads + last_grads
    pieces = [(step, [first_half]) for step in range(turns)]
    pieces += [(step, halves) for step in range(turns)]
    hidden_grad = backward(hidden_states, gain, grad_parts, pieces, turns, pair)

    for other in received:
        table = table + other.astype(jnp.float32)
    if near == 2:
        halves_at = dp_count // near
        arrived = to_share(table[halves_at:].astype(jnp.bfloat16), 1)
        table = table[:halves_at] + arrived.astype(jnp.float32)
    sent = table.astype(jnp.bfloat16)
    total = table[0]
    for step in range(dp_count - near, 0, -near):
        total = total + to_share(sent[step // near], step).astype(jnp.float32)
    error_mid = carried + total / dp_count
    error_sent = error_mid.astype(jnp.bfloat16)[None]
    error_sent, total = lax.optimization_barrier((error_sent, total))
    momentum_new = decayed + total / dp_count
    if near == 2:
        error_sent = jnp.concatenate([error_sent, from_share(error_sent, 1)], axis=0)
    parts = [error_sent] + [from_share(error_sent, step) for step in range(near, dp_count, near)]
    parts, hidden_grad = lax.optimization_barrier((parts, hidden_grad))
    update, error_new = unsketch(parts, rows, error_mid)
    return (
        hidden_grad,
        momentum_new.reshape(momentum.shape),
        error_new.reshape(error.shape),
        update,
    )


def solution(mesh):
    in_specs = (
        P(("dp", "fsdp"), None),
        P(),
        P("fsdp", None),
        P(("dp", "fsdp"), None),
        P(None, "fsdp"),
        P(None, "fsdp"),
        P("fsdp", None, "dp"),
        P("fsdp", None, "dp"),
    )
    out_specs = (
        P(("dp", "fsdp"), None),
        P("fsdp", None, "dp"),
        P("fsdp", None, "dp"),
        P("fsdp", None),
    )
    return jax.shard_map(
        on_device, mesh=mesh, in_specs=in_specs, out_specs=out_specs, check_vma=False
    )
```
